128 devices in a mesh: grp: 8 (over x, z_hi), rsp: 16 (over y, z_lo, core).
Axes of the slice: x: 4, y: 4, z: 4 (z_hi: 2, z_lo: 2; z = z_hi * 2 + z_lo), core: 2. Of those that a mesh axis runs over, the one named last changes fastest.
Arguments:
- prompt_x: bfloat16 [8192, 5120], P(('grp', 'rsp')), may hold values from -6 to 6
- key_value_weight: bfloat16 [5120, 1024], replicated, may hold values from -0.078125 to 0.078125
- queries: bfloat16 [32768, 4096], P(('grp', 'rsp')), may hold values from -90 to 90
- resp_kv: bfloat16 [32768, 1024], P(('grp', 'rsp')), may hold values from -6 to 6
- out_grad: bfloat16 [32768, 4096], P(('grp', 'rsp')), may hold values from -6 to 6
- lengths: int32 [256], P(('grp', 'rsp')), may hold values from 1 to 128, 24576 in all
- token_mask: int32 [256, 128], P(('grp', 'rsp')), may hold values 0 or 1
Outputs:
- query_grad: bfloat16 [32768, 4096], P(('grp', 'rsp'))
- resp_kv_grad: bfloat16 [32768, 1024], P(('grp', 'rsp'))
- prompt_x_grad: bfloat16 [8192, 5120], P(('grp', 'rsp'))
- w_kv_grad: float32 [5120, 1024], P('rsp')
The draws below stay inside these ranges and needn't reach their ends.
Inputs may be any that keep to these rules, and one draw needn't show every extreme that they name: `lengths`: between 1 and 128, the largest exactly 128.
All inputs are finite; a program needn't handle non-finite values. No bound on the sum of `lengths` or of `token_mask` on one device may be relied on, other than what follows from the above.
Results may differ from the reference program's by a relative error of at most 0.008.
Values may be sent and summed in bfloat16 or wider, within the bound.
A program may use at most 192 MiB of HBM per device.

```python
import math
import jax
import jax.numpy as jnp
import numpy as np
from jax import lax

MODEL_WIDTH = 5120
QUERY_HEADS = 32
KEY_VALUE_HEADS = 4
HEAD_WIDTH = 128
L = 128
P_SIZE = 1024
RESP = 32
RESPONSE_TOKENS = 32768
N_GRP = 8


def common_prompt_keys(key):
    return jnp.clip(jax.random.normal(key, (RESPONSE_TOKENS, 2 * KEY_VALUE_HEADS * HEAD_WIDTH), jnp.float32), -6.0, 6.0)


def draw_resp_kv(key, part):
    return common_prompt_keys(key).astype(jnp.bfloat16)


def draw_queries(key, part):
    key = jax.random.fold_in(key, 7)
    first_key = jax.random.fold_in(key, 0)
    values = jnp.clip(jax.random.normal(first_key, (RESPONSE_TOKENS, QUERY_HEADS * HEAD_WIDTH), jnp.float32), -6.0, 6.0)
    return values.astype(jnp.bfloat16)


def with_ends(array, own_key, low, top_value):
    dims = array.shape
    index_at = [jax.random.randint(jax.random.fold_in(own_key, axis), (), 0, dims[axis]) for axis in range(len(dims))]
    array = array.at[tuple(index_at)].set(low)
    longest = dims.index(max(dims))
    index_at[longest] = (index_at[longest] + 1) % dims[longest]
    return array.at[tuple(index_at)].set(top_value)


def block_scale(rng, shape, shards, low, largest):
    gain, own = 1.0, jax.random.fold_in(rng, 6)
    for axis_at, blocks in shards:
        draws = jnp.exp(jax.random.uniform(jax.random.fold_in(own, axis_at), (blocks,), jnp.float32, low / len(shards), largest / len(shards)))
        gain = gain * jnp.repeat(draws, shape[axis_at] // blocks).reshape([-1 if axis == axis_at else 1 for axis in range(len(shape))])
    return gain


def split_up(amount, total, limit, lean):
    loads = [(1 << 20) // math.isqrt(standing ** lean) + 1 for standing in range(2, amount + 1)]
    surplus, given = total - limit - (amount - 1), [1] * (amount - 1)
    while surplus > 0:
        movable = [i for i in range(amount - 1) if given[i] < limit]
        whole, left = sum([loads[i] for i in movable]), surplus
        for i in movable:
            more = min(limit - given[i], max(1, left * loads[i] // whole), surplus)
            given[i] = given[i] + more
            surplus = surplus - more
    return np.array([limit] + given)


def uneven(rng, number_of, total, most, lean):
    if number_of == 2:
        one = jax.random.randint(rng, (), max(1, total - most), min(most, total - 1) + 1)
        return jnp.stack([one, total - one])
    sizes = jnp.asarray(split_up(number_of, total, most, lean), jnp.int32)
    twos = (number_of - 1) // 2
    donor, taker = sizes[1:1 + 2 * twos:2], sizes[2:2 + 2 * twos:2]
    slack = jnp.minimum(donor - 1, most - taker)
    passed = jax.random.randint(jax.random.fold_in(rng, 1), (twos,), 0, 1 << 20) % (slack + 1)
    sizes = sizes.at[1:1 + 2 * twos:2].set(donor - passed).at[2:2 + 2 * twos:2].set(taker + passed)
    return sizes[jax.random.permutation(jax.random.fold_in(rng, 2), number_of)]


def gaussian(own_key, shape, spread, most, cuts=(), kind=jnp.bfloat16):
    drawn = jax.random.normal(own_key, shape, jnp.float32) * spread
    if len(cuts) > 0:
        drawn = block_scale(own_key, shape, cuts, -0.22, 0.18) * drawn
    return jnp.clip(drawn, min=-most, max=most).astype(kind)


def setup_inputs(seed: int = 0) -> dict:
    arg_keys = jax.random.split(jax.random.key(seed), 8)
    prompt_x = gaussian(arg_keys[0], (N_GRP * P_SIZE, MODEL_WIDTH), 1.0, 6.0, ((0, 128),))
    key_value_weight = gaussian(arg_keys[1], (MODEL_WIDTH, 2 * KEY_VALUE_HEADS * HEAD_WIDTH), MODEL_WIDTH ** -0.5, 0.078125)
    queries = draw_queries(jax.random.fold_in(arg_keys[7], 71), 0)
    resp_kv = draw_resp_kv(jax.random.fold_in(arg_keys[7], 71), 0)
    out_grad = gaussian(arg_keys[4], (RESPONSE_TOKENS, QUERY_HEADS * HEAD_WIDTH), 1.0, 6.0, ((0, 128),))
    lengths = uneven(arg_keys[5], N_GRP * RESP, N_GRP * RESP * L * 3 // 4, L, 1).astype(jnp.int32)
    token_mask = with_ends((jax.random.randint(arg_keys[6], (N_GRP * RESP, L), 0, 8) < 7).astype(jnp.int32), jax.random.fold_in(arg_keys[6], 1), 0, 1)
    return dict(prompt_x=prompt_x, key_value_weight=key_value_weight, queries=queries, resp_kv=resp_kv, out_grad=out_grad, lengths=lengths, token_mask=token_mask)


def head_terms(q_head, key_rows, value_rows, d_head, allowed, score_scale):
    q_full = q_head.astype(jnp.float32)
    key_full = key_rows.astype(jnp.float32)
    value_full = value_rows.astype(jnp.float32)
    d_full = d_head.astype(jnp.float32)
    scores = jnp.einsum('igd,jd->gij', q_full, key_full) * score_scale
    scores = jnp.where(allowed[None], scores, -1e30)
    row_max = jnp.max(scores, axis=-1, keepdims=True)
    exp_scores = jnp.exp(scores - row_max)
    attn_probs = exp_scores / jnp.sum(exp_scores, axis=-1, keepdims=True)
    probs_half = lax.optimization_barrier(attn_probs.astype(jnp.bfloat16)).astype(jnp.float32)
    value_grad = jnp.einsum('gij,igd->jd', probs_half, d_full)
    prob_grad = jnp.einsum('igd,jd->gij', d_full, value_full)
    center = jnp.sum(attn_probs * prob_grad, axis=-1, keepdims=True)
    score_grad = lax.optimization_barrier((attn_probs * (prob_grad - center)).astype(jnp.bfloat16)).astype(jnp.float32)
    q_grad = jnp.einsum('gij,jd->igd', score_grad, key_full) * score_scale
    key_grad = jnp.einsum('gij,igd->jd', score_grad, q_full) * score_scale
    return q_grad, key_grad, value_grad


def response_grads(prompt_kv, q_rows, own_kv, dout_rows, length, mask_row):
    key_value_width = KEY_VALUE_HEADS * HEAD_WIDTH
    heads_per_group = QUERY_HEADS // KEY_VALUE_HEADS
    score_scale = HEAD_WIDTH ** -0.5
    prompt_len = prompt_kv.shape[0]
    positions = jnp.arange(L, dtype=jnp.int32)
    columns = jnp.arange(prompt_len + L, dtype=jnp.int32) - prompt_len
    is_valid = (positions < length) & (mask_row == 1)
    allowed = (columns[None, :] < 0) | ((columns[None, :] <= positions[:, None]) & (columns[None, :] < length))
    d_rows = jnp.where(is_valid[:, None], dout_rows, jnp.zeros_like(dout_rows))
    q_parts, key_own, value_own, key_prompt, value_prompt = [], [], [], [], []
    for key_value_head in range(KEY_VALUE_HEADS):
        q_head = q_rows[:, key_value_head * heads_per_group * HEAD_WIDTH:(key_value_head + 1) * heads_per_group * HEAD_WIDTH].reshape(L, heads_per_group, HEAD_WIDTH)
        d_head = d_rows[:, key_value_head * heads_per_group * HEAD_WIDTH:(key_value_head + 1) * heads_per_group * HEAD_WIDTH].reshape(L, heads_per_group, HEAD_WIDTH)
        key_rows = jnp.concatenate([prompt_kv[:, key_value_head * HEAD_WIDTH:(key_value_head + 1) * HEAD_WIDTH], own_kv[:, key_value_head * HEAD_WIDTH:(key_value_head + 1) * HEAD_WIDTH]], 0)
        value_rows = jnp.concatenate([prompt_kv[:, key_value_width + key_value_head * HEAD_WIDTH:key_value_width + (key_value_head + 1) * HEAD_WIDTH], own_kv[:, key_value_width + key_value_head * HEAD_WIDTH:key_value_width + (key_value_head + 1) * HEAD_WIDTH]], 0)
        q_grad, key_grad, value_grad = head_terms(q_head, key_rows, value_rows, d_head, allowed, score_scale)
        q_parts.append(q_grad.reshape(L, heads_per_group * HEAD_WIDTH))
        key_own.append(key_grad[prompt_len:])
        value_own.append(value_grad[prompt_len:])
        key_prompt.append(key_grad[:prompt_len])
        value_prompt.append(value_grad[:prompt_len])
    query_grad = jnp.concatenate(q_parts, 1).astype(jnp.bfloat16)
    own_grad = jnp.concatenate(key_own + value_own, 1).astype(jnp.bfloat16)
    prompt_grad = jnp.concatenate(key_prompt + value_prompt, 1)
    return query_grad, own_grad, prompt_grad


def reference(prompt_x, key_value_weight, queries, resp_kv, out_grad, lengths, token_mask):
    key_value_width = KEY_VALUE_HEADS * HEAD_WIDTH
    prompt_kv = jnp.dot(prompt_x, key_value_weight, preferred_element_type=jnp.float32).astype(jnp.bfloat16)
    prompt_kv = prompt_kv.reshape(N_GRP, P_SIZE, 2 * key_value_width)

    def one_group(items):
        group_kv, group_q, group_own, group_dout, group_len, group_mask = items

        def one_response(state_sum, pieces):
            q_rows, own_kv, dout_rows, length, mask_row = pieces
            query_grad, own_grad, prompt_grad = response_grads(group_kv, q_rows, own_kv, dout_rows, length, mask_row)
            return state_sum + prompt_grad, (query_grad, own_grad)

        start_sum = jnp.zeros((P_SIZE, 2 * key_value_width), jnp.float32)
        total, outputs = lax.scan(one_response, start_sum, (group_q, group_own, group_dout, group_len, group_mask))
        return total, outputs[0], outputs[1]

    totals, q_out, own_out = lax.map(one_group, (
        prompt_kv,
        queries.reshape(N_GRP, RESP, L, QUERY_HEADS * HEAD_WIDTH),
        resp_kv.reshape(N_GRP, RESP, L, 2 * key_value_width),
        out_grad.reshape(N_GRP, RESP, L, QUERY_HEADS * HEAD_WIDTH),
        lengths.reshape(N_GRP, RESP),
        token_mask.reshape(N_GRP, RESP, L)))
    kv_grad_half = totals.astype(jnp.bfloat16).reshape(N_GRP * P_SIZE, 2 * key_value_width)
    prompt_x_grad = jnp.dot(kv_grad_half, key_value_weight.T, preferred_element_type=jnp.float32).astype(jnp.bfloat16)
    w_kv_grad = jnp.dot(prompt_x.T, kv_grad_half, preferred_element_type=jnp.float32)
    query_grad = q_out.reshape(RESPONSE_TOKENS, QUERY_HEADS * HEAD_WIDTH)
    resp_kv_grad = own_out.reshape(RESPONSE_TOKENS, 2 * key_value_width)
    return query_grad, resp_kv_grad, prompt_x_grad, w_kv_grad
```

```python
import functools

import jax
import jax.numpy as jnp
from jax import lax
from jax.experimental import pallas as pl
from jax.experimental.pallas import tpu as pltpu
from jax.sharding import PartitionSpec as P

HEADS = 4
PER = 8
D = 128
SEQ = 128
ROWS = PER * SEQ
PROMPT = 1024
KEYS = PROMPT + SEQ
TOK = 64
WIDTH = 5120
PEERS = 8
WROWS = 320
NX = 4
WPART = WROWS // NX
BF = jnp.bfloat16
F32 = jnp.float32
SCALE = D**-0.5
LOG2E = 1.4426950408889634
MESH = pl.DeviceIdType.MESH
NN = ((1,), (0,))
NT = ((1,), (1,))
TN = ((0,), (0,))


def dot(a, b, dims):
    return lax.dot_general(a, b, (dims, ((), ())), preferred_element_type=F32)


def lanes(start, size=D):
    return pl.ds(pl.multiple_of(start, D), size)


def kernel(
    x_hbm, w_hbm, q_hbm, kv_hbm, d_hbm, len_ref, mask_ref,
    qg, own_g, xg, wg,
    x, w, q, d, own,
    kv, pb, pr, rss, rsr, ga, xs, xr, ws, wr, zs, zr, wa,
    e0, s0, e1, s1, qd, r0, r1, xacc,
    in_sem, w_sem,
    kv_s, kv_r, kvp_s, kvp_r, p_s, p_r, rs_s, rs_r, ga_s, ga_r, gp_s, gp_r,
    x_s, x_r, w_s, w_r, z_s, z_r, wa_s, wa_r,
):
    g, r = lax.axis_index("grp"), lax.axis_index("rsp")
    core, at = r % 2, r // 2
    mate = at * 2 + 1 - core
    gx, gz = g // 2, g % 2
    z_mate = gx * 2 + 1 - gz
    mine = core * PEERS + at

    def remote(src, dst, send, recv, grp, rsp):
        return pltpu.make_async_remote_copy(
            src_ref=src, dst_ref=dst, send_sem=send, recv_sem=recv,
            device_id=(grp, rsp), device_id_type=MESH,
        )

    def each(count, f):
        def body(j, c):
            f(j)
            return c

        lax.fori_loop(1, count, body, 0)

    loads = [
        pltpu.make_async_copy(src, dst, in_sem.at[n])
        for n, (src, dst) in enumerate(((x_hbm, x), (q_hbm, q), (d_hbm, d), (kv_hbm, own)))
    ]

    def w_loads(h):
        return [
            pltpu.make_async_copy(
                w_hbm.at[:, pl.ds(t * 512 + h * D, D)], w.at[h, :, pl.ds(t * D, D)], w_sem.at[h, t]
            )
            for t in range(2)
        ]

    loads[0].start()
    for h in range(HEADS):
        for c in w_loads(h):
            c.start()
    for c in loads[1:]:
        c.start()

    barrier = pltpu.get_barrier_semaphore()
    each(16, lambda j: pl.semaphore_signal(
        barrier, inc=1, device_id=(g, (r + j) % 16), device_id_type=MESH))
    each(NX, lambda j: pl.semaphore_signal(
        barrier, inc=1, device_id=(((gx + j) % NX) * 2 + gz, r), device_id_type=MESH))
    pl.semaphore_signal(barrier, inc=1, device_id=(z_mate, r), device_id_type=MESH)

    def kv_copy(h, j, there):
        to = (at + j) % PEERS
        slot = core * PEERS + (to if there else at)
        return remote(kv.at[h, slot], kv.at[h, slot], kv_s.at[h, j],
                      kv_r.at[h, to if there else at], g, to * 2 + core)

    def kv_mate(h):
        half = kv.at[h, pl.ds(core * PEERS, PEERS)]
        return remote(half, half, kvp_s.at[h], kvp_r.at[h], g, mate)

    def kv_mate_in(h):
        half = kv.at[h, pl.ds((1 - core) * PEERS, PEERS)]
        return remote(half, half, kvp_s.at[h], kvp_r.at[h], g, mate)

    def p_copy(h):
        return remote(pb.at[h, pl.ds((1 - core) * PEERS, PEERS)], pr.at[h], p_s.at[h], p_r.at[h], g, mate)

    def rs_copy(h, j):
        to = (at + j) % PEERS
        return remote(rss.at[h, to], rsr.at[h, at], rs_s.at[h, j], rs_r.at[h, at], g, to * 2 + core)

    def rs_in(h, j):
        to = (at + j) % PEERS
        return remote(rss.at[h, to], rsr.at[h, to], rs_s.at[h, j], rs_r.at[h, to], g, to * 2 + core)

    def ga_copy(h, j, there):
        to = (at + j) % PEERS
        slot = core * PEERS + (to if there else at)
        return remote(ga.at[h, slot], ga.at[h, slot], ga_s.at[h, j],
                      ga_r.at[h, to if there else at], g, to * 2 + core)

    def ga_mate(h, side):
        half = ga.at[h, pl.ds(side * PEERS, PEERS)]
        return remote(half, half, gp_s.at[h], gp_r.at[h], g, mate)

    def x_copy(j):
        to = (r + j) % 16
        return remote(xs.at[to], xr.at[mine], x_s.at[j], x_r.at[mine], g, to)

    def x_in(j):
        to = (r + j) % 16
        slot = (to % 2) * PEERS + to // 2
        return remote(xs.at[to], xr.at[slot], x_s.at[j], x_r.at[slot], g, to)

    def w_copy(h, j):
        to = (gx + j) % NX
        return remote(ws.at[h, to], wr.at[h, gx], w_s.at[h, j], w_r.at[h, gx], to * 2 + gz, r)

    def w_in(h, j):
        to = (gx + j) % NX
        return remote(ws.at[h, to], wr.at[h, to], w_s.at[h, j], w_r.at[h, to], to * 2 + gz, r)

    def z_copy(h):
        return remote(zs.at[h], zr.at[h], z_s.at[h], z_r.at[h], z_mate, r)

    def wa_copy(h, j, there):
        to = (gx + j) % NX
        slot = to if there else gx
        return remote(wa.at[h, slot], wa.at[h, slot], wa_s.at[h, j], wa_r.at[h, slot], to * 2 + gz, r)

    loads[0].wait()
    for h in range(HEADS):
        for c in w_loads(h):
            c.wait()
        kv[h, mine] = dot(x[...], w[h], NN).astype(BF)
        if h == 0:
            pl.semaphore_wait(barrier, 15 + NX)
        each(PEERS, lambda j, h=h: kv_copy(h, j, False).start())
    for to in range(16):
        xs[to] = x[:, to * WROWS:(to + 1) * WROWS]
    xr[mine] = xs[r]

    for c in loads[1:]:
        c.wait()
    row = lax.broadcasted_iota(jnp.int32, (SEQ, D), 0)
    for n in range(2):
        live = jnp.broadcast_to(mask_ref[n:n + 1, :].astype(F32), (SEQ, SEQ)).T
        live = (live == 1.0) & (row < len_ref[n])
        rows = slice(n * SEQ, (n + 1) * SEQ)

        def clear(c, _, rows=rows, live=live):
            cols = lanes(c * D)
            d[rows, cols] = jnp.where(live, d[rows, cols].astype(F32), 0.0).astype(BF)
            return _

        lax.fori_loop(0, HEADS * PER, clear, 0)

    def kv_relay(h):
        each(PEERS, lambda j: kv_copy(h, j, True).wait_recv())
        kv_mate(h).start()

    kv_relay(0)
    each(16, lambda j: x_copy(j).start())

    es, ss, rr = (e0, e1), (s0, s1), (r0, r1)
    causal = (lax.broadcasted_iota(jnp.int32, (ROWS, SEQ), 1)
              <= lax.broadcasted_iota(jnp.int32, (ROWS, SEQ), 0) % SEQ)

    def own_kv(h, n):
        rows = slice(n * SEQ, (n + 1) * SEQ)
        return own[rows, lanes(h * D)], own[rows, lanes(512 + h * D)]

    def softmax_part(h, n):
        rows = slice(n * SEQ, (n + 1) * SEQ)
        qn = jnp.concatenate([q[rows, lanes((h * PER + t) * D)] for t in range(PER)], 0)
        dn = jnp.concatenate([d[rows, lanes((h * PER + t) * D)] for t in range(PER)], 0)
        keys = kv[h, :, :, 0:D].reshape(PROMPT, D)
        values = kv[h, :, :, D:].reshape(PROMPT, D)
        ko, vo = own_kv(h, n)
        none = jnp.zeros_like(ko)
        both = jnp.concatenate(
            [jnp.concatenate([ko, none], 1), jnp.concatenate([none, vo], 1)], 0)
        last = dot(jnp.concatenate([qn, dn], 1), both, NT)
        scores = jnp.concatenate(
            [dot(qn, keys, NT), jnp.where(causal, last[:, :SEQ], -1e30)], 1)
        pgrad = jnp.concatenate([dot(dn, values, NT), last[:, SEQ:]], 1)
        top = jnp.max(scores, axis=1, keepdims=True)
        e = jnp.exp2((scores - top) * (SCALE * LOG2E))
        inv = 1.0 / jnp.sum(e, axis=1, keepdims=True)
        center = jnp.sum(e * pgrad, axis=1, keepdims=True) * inv
        es[n][...] = e.astype(BF)
        ss[n][...] = (e * (pgrad - center)).astype(BF)
        rr[n][...] = jnp.broadcast_to(inv, (ROWS, D))
        qd[n, :, 0:D] = (qn * inv).astype(BF)
        qd[n, :, D:] = (dn * inv).astype(BF)

    def key_part(h):
        total = []
        for n in range(2):
            dk = dot(qd[n, :, 0:D], ss[n][...], TN) * SCALE
            dv = dot(qd[n, :, D:], es[n][...], TN)
            rows = slice(n * SEQ, (n + 1) * SEQ)
            own_g[rows, lanes(h * D)] = dk[:, PROMPT:].astype(BF).T
            own_g[rows, lanes(512 + h * D)] = dv[:, PROMPT:].astype(BF).T
            total.append((dk[:, :PROMPT], dv[:, :PROMPT]))
        dk, dv = total[0][0] + total[1][0], total[0][1] + total[1][1]
        pb[h, :, :, 0:D] = dk.astype(BF).T.reshape(16, TOK, D)
        pb[h, :, :, D:] = dv.astype(BF).T.reshape(16, TOK, D)

    def query_part(h, n):
        rows = slice(n * SEQ, (n + 1) * SEQ)
        keys = jnp.concatenate([kv[h, :, :, 0:D].reshape(PROMPT, D), own_kv(h, n)[0]], 0)
        out = (dot(ss[n][...], keys, NN) * (rr[n][...] * SCALE)).astype(BF)
        for t in range(PER):
            qg[rows, lanes((h * PER + t) * D)] = out[t * SEQ:(t + 1) * SEQ]

    def pair_sum(h):
        p_copy(h).wait_recv()
        half = pb[h, pl.ds(core * PEERS, PEERS)].astype(F32) + pr[h].astype(F32)
        rss[h] = half.astype(BF)
        rsr[h, at] = rss[h, at]
        each(PEERS, lambda j: rs_copy(h, j).start())

    def group_sum(h):
        each(PEERS, lambda j: rs_in(h, j).wait_recv())
        total = rsr[h, 0].astype(F32)
        for j in range(1, PEERS):
            total += rsr[h, j].astype(F32)
        ga[h, mine] = total.astype(BF)
        each(PEERS, lambda j: ga_copy(h, j, False).start())

    def spread(h):
        each(PEERS, lambda j: ga_copy(h, j, True).wait_recv())
        ga_mate(h, core).start()

    def x_part(h):
        def tile(c, _):
            rows = pl.ds(c * 1024, 1024)
            xacc[:, lanes(c * 1024, 1024)] += dot(ga[h, mine], w[h, rows, :], NT)
            return _

        lax.fori_loop(0, WIDTH // 1024, tile, 0)

    def w_part(h):
        ga_mate(h, 1 - core).wait_recv()
        part = dot(xr[...].reshape(PROMPT, WROWS), ga[h].reshape(PROMPT, 2 * D), TN)
        ws[h] = part.astype(BF).reshape(NX, WPART, 2 * D)
        wr[h, gx] = ws[h, gx]
        each(NX, lambda j: w_copy(h, j).start())

    def w_sum(h):
        each(NX, lambda j: w_in(h, j).wait_recv())
        total = wr[h, 0].astype(F32)
        for j in range(1, NX):
            total += wr[h, j].astype(F32)
        zs[h] = total.astype(BF)
        z_copy(h).start()

    def z_sum(h):
        z_copy(h).wait_recv()
        wa[h, gx] = (zs[h].astype(F32) + zr[h].astype(F32)).astype(BF)
        each(NX, lambda j: wa_copy(h, j, False).start())

    def w_out(h):
        each(NX, lambda j: wa_copy(h, j, True).wait_recv())
        full = wa[h].astype(F32).reshape(WROWS, 2 * D)
        wg[:, lanes(h * D)] = full[:, :D]
        wg[:, lanes(512 + h * D)] = full[:, D:]

    xacc[...] = jnp.zeros_like(xacc)

    def head(h, c):
        kv_mate_in(h).wait_recv()
        softmax_part(h, 0)

        @pl.when(h >= 1)
        def _():
            group_sum(h - 1)

        @pl.when(h >= 2)
        def _():
            w_sum(h - 2)

        @pl.when(h < HEADS - 1)
        def _():
            kv_relay(h + 1)

        softmax_part(h, 1)

        @pl.when(h == 0)
        def _():
            each(16, lambda j: x_in(j).wait_recv())

        @pl.when(h >= 1)
        def _():
            spread(h - 1)

        @pl.when(h >= 2)
        def _():
            z_sum(h - 2)

        key_part(h)
        p_copy(h).start()

        @pl.when(h >= 1)
        def _():
            x_part(h - 1)
            w_part(h - 1)

        pair_sum(h)
        query_part(h, 0)
        query_part(h, 1)

        @pl.when(h >= 2)
        def _():
            w_out(h - 2)

        return c

    lax.fori_loop(0, HEADS, head, 0)

    last = HEADS - 1
    w_sum(last - 1)
    group_sum(last)
    z_sum(last - 1)
    x_part(last)
    spread(last)
    xg[...] = xacc[...].astype(BF)
    w_out(last - 1)
    w_part(last)
    w_sum(last)
    z_sum(last)

    def sent(h, c):
        each(PEERS, lambda j: kv_copy(h, j, False).wait_send())
        kv_mate(h).wait_send()
        p_copy(h).wait_send()
        each(PEERS, lambda j: rs_copy(h, j).wait_send())
        each(PEERS, lambda j: ga_copy(h, j, False).wait_send())
        ga_mate(h, core).wait_send()
        each(NX, lambda j: w_copy(h, j).wait_send())
        z_copy(h).wait_send()
        each(NX, lambda j: wa_copy(h, j, False).wait_send())
        return c

    w_out(last)
    lax.fori_loop(0, HEADS, sent, 0)
    each(16, lambda j: x_copy(j).wait_send())


def local(prompt_x, key_value_weight, queries, resp_kv, out_grad, lengths, token_mask):
    dma = pltpu.SemaphoreType.DMA
    vmem = pl.BlockSpec(memory_space=pltpu.VMEM)
    hbm = pl.BlockSpec(memory_space=pl.ANY)
    pairs = lambda *shape: [dma(shape), dma(shape)]
    return pl.pallas_call(
        kernel,
        out_shape=(
            jax.ShapeDtypeStruct((2 * SEQ, HEADS * PER * D), BF),
            jax.ShapeDtypeStruct((2 * SEQ, 2 * HEADS * D), BF),
            jax.ShapeDtypeStruct((TOK, WIDTH), BF),
            jax.ShapeDtypeStruct((WROWS, 2 * HEADS * D), F32),
        ),
        in_specs=[hbm] * 5 + [pl.BlockSpec(memory_space=pltpu.SMEM), vmem],
        out_specs=(vmem,) * 4,
        scratch_shapes=[
            pltpu.VMEM((TOK, WIDTH), BF),
            pltpu.VMEM((HEADS, WIDTH, 2 * D), BF),
            pltpu.VMEM((2 * SEQ, HEADS * PER * D), BF),
            pltpu.VMEM((2 * SEQ, HEADS * PER * D), BF),
            pltpu.VMEM((2 * SEQ, 2 * HEADS * D), BF),
            pltpu.VMEM((HEADS, 16, TOK, 2 * D), BF),
            pltpu.VMEM((HEADS, 16, TOK, 2 * D), BF),
            pltpu.VMEM((HEADS, PEERS, TOK, 2 * D), BF),
            pltpu.VMEM((HEADS, PEERS, TOK, 2 * D), BF),
            pltpu.VMEM((HEADS, PEERS, TOK, 2 * D), BF),
            pltpu.VMEM((HEADS, 16, TOK, 2 * D), BF),
            pltpu.VMEM((16, TOK, WROWS), BF),
            pltpu.VMEM((16, TOK, WROWS), BF),
            pltpu.VMEM((HEADS, NX, WPART, 2 * D), BF),
            pltpu.VMEM((HEADS, NX, WPART, 2 * D), BF),
            pltpu.VMEM((HEADS, WPART, 2 * D), BF),
            pltpu.VMEM((HEADS, WPART, 2 * D), BF),
            pltpu.VMEM((HEADS, NX, WPART, 2 * D), BF),
            pltpu.VMEM((ROWS, KEYS), BF),
            pltpu.VMEM((ROWS, KEYS), BF),
            pltpu.VMEM((ROWS, KEYS), BF),
            pltpu.VMEM((ROWS, KEYS), BF),
            pltpu.VMEM((2, ROWS, 2 * D), BF),
            pltpu.VMEM((ROWS, D), F32),
            pltpu.VMEM((ROWS, D), F32),
            pltpu.VMEM((TOK, WIDTH), F32),
            dma((4,)),
            dma((HEADS, 2)),
            *pairs(HEADS, PEERS),
            *pairs(HEADS),
            *pairs(HEADS),
            *pairs(HEADS, PEERS),
            *pairs(HEADS, PEERS),
            *pairs(HEADS),
            *pairs(16),
            *pairs(HEADS, NX),
            *pairs(HEADS),
            *pairs(HEADS, NX),
        ],
        compiler_params=pltpu.CompilerParams(
            collective_id=0, has_side_effects=True, vmem_limit_bytes=62 << 20
        ),
    )(prompt_x, key_value_weight, queries, resp_kv, out_grad, lengths, token_mask)


def solution(mesh):
    rows = P(("grp", "rsp"), None)
    return jax.shard_map(
        local,
        mesh=mesh,
        in_specs=(rows, P(), rows, rows, rows, P(("grp", "rsp")), rows),
        out_specs=(rows, rows, rows, P("rsp", None)),
        check_vma=False,
    )
```

```python
import functools

import jax
import jax.numpy as jnp
from jax import lax
from jax.experimental import pallas as pl
from jax.experimental.pallas import tpu as pltpu
from jax.sharding import PartitionSpec as P

HEADS = 4
PER = 8
D = 128
SEQ = 128
ROWS = PER * SEQ
PROMPT = 1024
KEYS = PROMPT + SEQ
TOK = 64
WIDTH = 5120
PEERS = 8
WROWS = 320
GRPS = 8
WPART = 80
KEPT = 2
BF = jnp.bfloat16
F32 = jnp.float32
SCALE = D**-0.5
LOG2E = 1.4426950408889634
MESH = pl.DeviceIdType.MESH
NN = ((1,), (0,))
NT = ((1,), (1,))
TN = ((0,), (0,))


def dot(a, b, dims):
    return lax.dot_general(a, b, (dims, ((), ())), preferred_element_type=F32)


def lanes(start, size=D):
    return pl.ds(pl.multiple_of(start, D), size)


def kernel(
    x_hbm, w_hbm, q_hbm, kv_hbm, d_hbm, len_ref, mask_ref,
    qg_hbm, own_hbm, xg_hbm, wa_hbm,
    x, w, q, d, own, qg, own_g, xg,
    kv, pb, pr, rsr, ga, xr, wf, wp, ws, wr, wa,
    es, ss, rr, qd, xacc,
    in_sem, w_sem, qg_sem, out_sem,
    kv_s, kv_r, kvp_s, kvp_r, p_s, p_r, rs_s, rs_r, ga_s, ga_r,
    x_s, x_r, wp_s, wp_r, w_s, w_r, wa_s, wa_r,
):
    g, r = lax.axis_index("grp"), lax.axis_index("rsp")
    core, at = r % 2, r // 2
    mate = at * 2 + 1 - core
    mine = core * PEERS + at

    def remote(src, dst, send, recv, grp, rsp):
        return pltpu.make_async_remote_copy(
            src_ref=src, dst_ref=dst, send_sem=send, recv_sem=recv,
            device_id=(grp, rsp), device_id_type=MESH,
        )

    def each(count, f):
        def body(j, c):
            f(j)
            return c

        lax.fori_loop(1, count, body, 0)

    loads = [
        pltpu.make_async_copy(src, dst, in_sem.at[n])
        for n, (src, dst) in enumerate(((x_hbm, x), (q_hbm, q), (d_hbm, d), (kv_hbm, own)))
    ]

    def w_loads(h):
        return [
            pltpu.make_async_copy(
                w_hbm.at[:, pl.ds(t * 512 + h * D, D)], w.at[h, :, pl.ds(t * D, D)], w_sem.at[h, t]
            )
            for t in range(2)
        ]

    barrier = pltpu.get_barrier_semaphore()
    each(16, lambda j: pl.semaphore_signal(
        barrier, inc=1, device_id=(g, (r + j) % 16), device_id_type=MESH))
    each(GRPS, lambda j: pl.semaphore_signal(
        barrier, inc=1, device_id=((g + j) % GRPS, r), device_id_type=MESH))

    loads[0].start()
    for h in range(HEADS):
        for c in w_loads(h):
            c.start()
        if h == 1:
            for c in loads[1:]:
                c.start()

    def kv_copy(h, j, there):
        to = (at + j) % PEERS
        slot = core * PEERS + (to if there else at)
        return remote(kv.at[h, slot], kv.at[h, slot], kv_s.at[h, j],
                      kv_r.at[h, to if there else at], g, to * 2 + core)

    def kv_mate(h, side):
        half = kv.at[h, pl.ds(side * PEERS, PEERS)]
        return remote(half, half, kvp_s.at[h], kvp_r.at[h], g, mate)

    def p_copy(h):
        return remote(pb.at[h, pl.ds((1 - core) * PEERS, PEERS)], pr.at[h], p_s.at[h], p_r.at[h], g, mate)

    def rs_copy(h, j, there):
        to = (at + j) % PEERS
        slot = to if there else at
        return remote(pb.at[h, core * PEERS + to], rsr.at[h, slot], rs_s.at[h, j], rs_r.at[h, slot],
                      g, to * 2 + core)

    def ga_copy(h, j, there):
        to = (at + j) % PEERS
        slot = to if there else at
        return remote(ga.at[h, slot], ga.at[h, slot], ga_s.at[h, j], ga_r.at[h, slot], g, to * 2 + core)

    def x_cols(place):
        return lanes(place * 2 * WROWS, 2 * WROWS)

    def x_copy(j, there):
        to = (at + j) % PEERS
        slot = to if there else at
        return remote(x.at[:, x_cols(to)], xr.at[slot], x_s.at[j], x_r.at[slot], g, to * 2 + core)

    def wp_copy(h):
        return remote(wf.at[h, 1 - core], wp.at[h], wp_s.at[h], wp_r.at[h], g, mate)

    def w_copy(h, j, there):
        to = (g + j) % GRPS
        slot = to if there else g
        return remote(ws.at[h, to], wr.at[h, slot], w_s.at[h, j], w_r.at[h, slot], to, r)

    def wa_copy(h, j, there):
        to = (g + j) % GRPS
        slot = to if there else g
        return remote(wa.at[h, slot], wa.at[h, slot], wa_s.at[h, j], wa_r.at[h, slot], to, r)

    def kv_send(h):
        each(PEERS, lambda j: kv_copy(h, j, False).start())

    def kv_relay(h):
        each(PEERS, lambda j: kv_copy(h, j, True).wait_recv())
        kv_mate(h, core).start()

    loads[0].wait()
    for h in range(HEADS):
        for c in w_loads(h):
            c.wait()
        kv[h, mine] = dot(x[...], w[h], NN).astype(BF)
        if h == 0:
            pl.semaphore_wait(barrier, 15 + GRPS - 1)
            kv_send(0)

    for c in loads[1:]:
        c.wait()
    row = lax.broadcasted_iota(jnp.int32, (SEQ, D), 0)
    for n in range(2):
        live = jnp.broadcast_to(mask_ref[n:n + 1, :].astype(F32), (SEQ, SEQ)).T
        live = (live == 1.0) & (row < len_ref[n])
        rows = slice(n * SEQ, (n + 1) * SEQ)

        def clear(c, _, rows=rows, live=live):
            cols = lanes(c * D)
            d[rows, cols] = jnp.where(live, d[rows, cols].astype(F32), 0.0).astype(BF)
            return _

        lax.fori_loop(0, HEADS * PER, clear, 0)
    xr[at] = x[:, x_cols(at)]
    xacc[...] = jnp.zeros_like(xacc)

    kv_relay(0)
    kv_send(1)

    causal = (lax.broadcasted_iota(jnp.int32, (ROWS, SEQ), 1)
              <= lax.broadcasted_iota(jnp.int32, (ROWS, SEQ), 0) % SEQ)

    def own_kv(h, n):
        rows = slice(n * SEQ, (n + 1) * SEQ)
        return own[rows, lanes(h * D)], own[rows, lanes(512 + h * D)]

    def kept(h, n):
        return (h % KEPT) * 2 + n

    def softmax_part(h, n):
        rows = slice(n * SEQ, (n + 1) * SEQ)
        qn = jnp.concatenate([q[rows, lanes((h * PER + t) * D)] for t in range(PER)], 0)
        dn = jnp.concatenate([d[rows, lanes((h * PER + t) * D)] for t in range(PER)], 0)
        keys = kv[h, :, :, 0:D].reshape(PROMPT, D)
        values = kv[h, :, :, D:].reshape(PROMPT, D)
        ko, vo = own_kv(h, n)
        none = jnp.zeros_like(ko)
        both = jnp.concatenate(
            [jnp.concatenate([ko, none], 1), jnp.concatenate([none, vo], 1)], 0)
        last = dot(jnp.concatenate([qn, dn], 1), both, NT)
        scores = jnp.concatenate(
            [dot(qn, keys, NT), jnp.where(causal, last[:, :SEQ], -1e30)], 1)
        pgrad = jnp.concatenate([dot(dn, values, NT), last[:, SEQ:]], 1)
        top = jnp.max(scores, axis=1, keepdims=True)
        e = jnp.exp2((scores - top) * (SCALE * LOG2E))
        inv = 1.0 / jnp.sum(e, axis=1, keepdims=True)
        center = jnp.sum(e * pgrad, axis=1, keepdims=True) * inv
        es[n] = e.astype(BF)
        ss[kept(h, n)] = (e * (pgrad - center)).astype(BF)
        rr[kept(h, n)] = jnp.broadcast_to(inv, (ROWS, D))
        qd[n, :, 0:D] = (qn * inv).astype(BF)
        qd[n, :, D:] = (dn * inv).astype(BF)

    def key_part(h):
        total = []
        for n in range(2):
            dk = dot(qd[n, :, 0:D], ss[kept(h, n)], TN) * SCALE
            dv = dot(qd[n, :, D:], es[n], TN)
            rows = slice(n * SEQ, (n + 1) * SEQ)
            own_g[rows, lanes(h * D)] = dk[:, PROMPT:].astype(BF).T
            own_g[rows, lanes(512 + h * D)] = dv[:, PROMPT:].astype(BF).T
            total.append((dk[:, :PROMPT], dv[:, :PROMPT]))
        dk, dv = total[0][0] + total[1][0], total[0][1] + total[1][1]
        pb[h, :, :, 0:D] = dk.astype(BF).T.reshape(16, TOK, D)
        pb[h, :, :, D:] = dv.astype(BF).T.reshape(16, TOK, D)

    def qg_out(h, n):
        part = (pl.ds(n * SEQ, SEQ), lanes(h * PER * D, PER * D))
        return pltpu.make_async_copy(qg.at[part], qg_hbm.at[part], qg_sem.at[h, n])

    def query_part(h, n):
        rows = slice(n * SEQ, (n + 1) * SEQ)
        keys = jnp.concatenate([kv[h, :, :, 0:D].reshape(PROMPT, D), own_kv(h, n)[0]], 0)
        out = (dot(ss[kept(h, n)], keys, NN) * (rr[kept(h, n)] * SCALE)).astype(BF)
        for t in range(PER):
            qg[rows, lanes((h * PER + t) * D)] = out[t * SEQ:(t + 1) * SEQ]
        qg_out(h, n).start()

    def pair_sum(h):
        p_copy(h).wait_recv()
        half = pb[h, pl.ds(core * PEERS, PEERS)].astype(F32) + pr[h].astype(F32)
        pb[h, pl.ds(core * PEERS, PEERS)] = half.astype(BF)
        each(PEERS, lambda j: rs_copy(h, j, False).start())
        rsr[h, at] = pb[h, mine]

    def group_sum(h):
        each(PEERS, lambda j: rs_copy(h, j, True).wait_recv())
        total = rsr[h, 0].astype(F32)
        for j in range(1, PEERS):
            total += rsr[h, j].astype(F32)
        ga[h, at] = total.astype(BF)
        each(PEERS, lambda j: ga_copy(h, j, False).start())

    def x_part(h):
        def tile(c, _):
            rows = pl.ds(c * 1024, 1024)
            xacc[:, lanes(c * 1024, 1024)] += dot(ga[h, at], w[h, rows, :], NT)
            return _

        lax.fori_loop(0, WIDTH // 1024, tile, 0)

    def w_part(h):
        each(PEERS, lambda j: ga_copy(h, j, True).wait_recv())
        part = dot(xr[...].reshape(PEERS * TOK, 2 * WROWS), ga[h].reshape(PEERS * TOK, 2 * D), TN)
        wf[h] = part.reshape(2, WROWS, 2 * D)
        wp_copy(h).start()

    def w_pair(h):
        wp_copy(h).wait_recv()
        part = (wf[h, core] + wp[h]).astype(BF)
        for i in range(4):
            for t in range(2):
                ws[h, i * 2 + t] = part[i * WPART:(i + 1) * WPART, t * D:(t + 1) * D]
        each(GRPS, lambda j: w_copy(h, j, False).start())
        wr[h, g] = ws[h, g]

    def w_sum(h):
        each(GRPS, lambda j: w_copy(h, j, True).wait_recv())
        total = wr[h, 0].astype(F32)
        for j in range(1, GRPS):
            total += wr[h, j].astype(F32)
        wa[h, g] = total.astype(BF)
        each(GRPS, lambda j: wa_copy(h, j, False).start())

    def wa_out(h):
        return pltpu.make_async_copy(wa.at[h], wa_hbm.at[h], out_sem.at[2 + h])

    def w_out(h):
        each(GRPS, lambda j: wa_copy(h, j, True).wait_recv())
        wa_out(h).start()

    def head(h, c):
        @pl.when(h >= 1)
        def _():
            kv_mate(h, 1 - core).wait_recv()

        @pl.when(h == 0)
        def _():
            kv_mate(0, 1 - core).wait_recv()

        softmax_part(h, 0)

        @pl.when(h >= 1)
        def _():
            pair_sum(h - 1)

        @pl.when(h < HEADS - 2)
        def _():
            kv_send(h + 2)

        softmax_part(h, 1)

        @pl.when(h < HEADS - 1)
        def _():
            kv_relay(h + 1)

        @pl.when(h >= 2)
        def _():
            group_sum(h - 2)

        key_part(h)
        p_copy(h).start()

        @pl.when(h == 0)
        def _():
            each(PEERS, lambda j: x_copy(j, False).start())

        @pl.when(h < HEADS - KEPT)
        def _():
            query_part(h, 0)
            query_part(h, 1)

        return c

    lax.fori_loop(0, HEADS, head, 0)

    own_out = pltpu.make_async_copy(own_g, own_hbm, out_sem.at[0])
    xg_out = pltpu.make_async_copy(xg, xg_hbm, out_sem.at[1])
    own_out.start()
    query_part(2, 0)
    pair_sum(3)
    group_sum(2)
    each(PEERS, lambda j: x_copy(j, True).wait_recv())
    w_part(0)
    query_part(2, 1)
    w_pair(0)
    w_part(1)
    x_part(0)
    w_pair(1)
    x_part(1)
    group_sum(3)
    x_part(2)
    w_sum(0)
    w_part(2)
    query_part(3, 0)
    w_pair(2)
    w_sum(1)
    query_part(3, 1)
    w_part(3)
    x_part(3)
    xg[...] = xacc[...].astype(BF)
    xg_out.start()
    w_pair(3)
    w_sum(2)
    w_out(0)
    w_out(1)
    w_sum(3)
    w_out(2)

    def sent(h, c):
        each(PEERS, lambda j: kv_copy(h, j, False).wait_send())
        kv_mate(h, core).wait_send()
        p_copy(h).wait_send()
        each(PEERS, lambda j: rs_copy(h, j, False).wait_send())
        each(PEERS, lambda j: ga_copy(h, j, False).wait_send())
        wp_copy(h).wait_send()
        each(GRPS, lambda j: w_copy(h, j, False).wait_send())
        for n in range(2):
            qg_out(h, n).wait()
        return c

    lax.fori_loop(0, HEADS, sent, 0)
    each(PEERS, lambda j: x_copy(j, False).wait_send())
    own_out.wait()
    xg_out.wait()
    w_out(3)

    def gathered(h, c):
        each(GRPS, lambda j: wa_copy(h, j, False).wait_send())
        return c

    lax.fori_loop(0, HEADS, gathered, 0)
    for h in range(HEADS):
        wa_out(h).wait()


def finish(qg_in, own_in, xg_in, wa, qg, own_g, xg, wg, sem):
    copies = [
        pltpu.make_async_copy(src, dst, sem.at[n])
        for n, (src, dst) in enumerate(((qg_in, qg), (own_in, own_g), (xg_in, xg)))
    ]
    for c in copies:
        c.start()
    for h in range(HEADS):
        for i in range(4):
            for t in range(2):
                wg[i * WPART:(i + 1) * WPART, t * 512 + h * D:t * 512 + (h + 1) * D] = (
                    wa[h, i * 2 + t].astype(F32))
    for c in copies:
        c.wait()


def local(prompt_x, key_value_weight, queries, resp_kv, out_grad, lengths, token_mask):
    dma = pltpu.SemaphoreType.DMA
    vmem = pl.BlockSpec(memory_space=pltpu.VMEM)
    hbm = pl.BlockSpec(memory_space=pl.ANY)
    pairs = lambda *shape: [dma(shape), dma(shape)]
    qg_shape = jax.ShapeDtypeStruct((2 * SEQ, HEADS * PER * D), BF)
    own_shape = jax.ShapeDtypeStruct((2 * SEQ, 2 * HEADS * D), BF)
    xg_shape = jax.ShapeDtypeStruct((TOK, WIDTH), BF)
    parts = pl.pallas_call(
        kernel,
        out_shape=(
            qg_shape, own_shape, xg_shape,
            jax.ShapeDtypeStruct((HEADS, GRPS, WPART, D), BF),
        ),
        in_specs=[hbm] * 5 + [pl.BlockSpec(memory_space=pltpu.SMEM), vmem],
        out_specs=(hbm,) * 4,
        scratch_shapes=[
            pltpu.VMEM((TOK, WIDTH), BF),
            pltpu.VMEM((HEADS, WIDTH, 2 * D), BF),
            pltpu.VMEM((2 * SEQ, HEADS * PER * D), BF),
            pltpu.VMEM((2 * SEQ, HEADS * PER * D), BF),
            pltpu.VMEM((2 * SEQ, 2 * HEADS * D), BF),
            pltpu.VMEM((2 * SEQ, HEADS * PER * D), BF),
            pltpu.VMEM((2 * SEQ, 2 * HEADS * D), BF),
            pltpu.VMEM((TOK, WIDTH), BF),
            pltpu.VMEM((HEADS, 16, TOK, 2 * D), BF),
            pltpu.VMEM((HEADS, 16, TOK, 2 * D), BF),
            pltpu.VMEM((HEADS, PEERS, TOK, 2 * D), BF),
            pltpu.VMEM((HEADS, PEERS, TOK, 2 * D), BF),
            pltpu.VMEM((HEADS, PEERS, TOK, 2 * D), BF),
            pltpu.VMEM((PEERS, TOK, 2 * WROWS), BF),
            pltpu.VMEM((HEADS, 2, WROWS, 2 * D), F32),
            pltpu.VMEM((HEADS, WROWS, 2 * D), F32),
            pltpu.VMEM((HEADS, GRPS, WPART, D), BF),
            pltpu.VMEM((HEADS, GRPS, WPART, D), BF),
            pltpu.VMEM((HEADS, GRPS, WPART, D), BF),
            pltpu.VMEM((2, ROWS, KEYS), BF),
            pltpu.VMEM((2 * KEPT, ROWS, KEYS), BF),
            pltpu.VMEM((2 * KEPT, ROWS, D), F32),
            pltpu.VMEM((2, ROWS, 2 * D), BF),
            pltpu.VMEM((TOK, WIDTH), F32),
            dma((4,)),
            dma((HEADS, 2)),
            dma((HEADS, 2)),
            dma((2 + HEADS,)),
            *pairs(HEADS, PEERS),
            *pairs(HEADS),
            *pairs(HEADS),
            *pairs(HEADS, PEERS),
            *pairs(HEADS, PEERS),
            *pairs(PEERS),
            *pairs(HEADS),
            *pairs(HEADS, GRPS),
            *pairs(HEADS, GRPS),
        ],
        compiler_params=pltpu.CompilerParams(
            collective_id=0, has_side_effects=True, vmem_limit_bytes=63 << 20
        ),
    )(prompt_x, key_value_weight, queries, resp_kv, out_grad, lengths, token_mask)
    return pl.pallas_call(
        finish,
        out_shape=(
            qg_shape, own_shape, xg_shape,
            jax.ShapeDtypeStruct((WROWS, 2 * HEADS * D), F32),
        ),
        in_specs=[hbm] * 3 + [vmem],
        out_specs=(hbm,) * 3 + (vmem,),
        scratch_shapes=[dma((3,))],
    )(*parts)


def solution(mesh):
    rows = P(("grp", "rsp"), None)
    return jax.shard_map(
        local,
        mesh=mesh,
        in_specs=(rows, P(), rows, rows, rows, P(("grp", "rsp")), rows),
        out_specs=(rows, rows, rows, P("rsp", None)),
        check_vma=False,
    )
```

```python
import functools

import jax
import jax.numpy as jnp
from jax import lax
from jax.experimental import pallas as pl
from jax.experimental.pallas import tpu as pltpu
from jax.sharding import PartitionSpec as P

HEADS = 4
PER = 8
D = 128
SEQ = 128
ROWS = PER * SEQ
PROMPT = 1024
KEYS = PROMPT + SEQ
TOK = 64
WIDTH = 5120
PEERS = 8
WROWS = 320
GRPS = 8
NX = 4
WPART = WROWS // NX
KEPT = 4
BF = jnp.bfloat16
F32 = jnp.float32
SCALE = D**-0.5
LOG2E = 1.4426950408889634
MESH = pl.DeviceIdType.MESH
NN = ((1,), (0,))
NT = ((1,), (1,))
TN = ((0,), (0,))


def dot(a, b, dims):
    return lax.dot_general(a, b, (dims, ((), ())), preferred_element_type=F32)


def lanes(start, size=D):
    return pl.ds(pl.multiple_of(start, D), size)


def kernel(
    x_hbm, w_hbm, q_hbm, kv_hbm, d_hbm, len_ref, mask_ref,
    qg_hbm, own_hbm, xg_hbm, wa_hbm,
    x, w, q, d, own, own_g,
    kv, pb, pr, rsr, ga, xr, wf, wo, wp, ws, wr, zs, zr, wa, wz,
    es, ss, dd, xacc,
    in_sem, w_sem, qg_sem, out_sem,
    kv_s, kv_r, kvp_s, kvp_r, p_s, p_r, rs_s, rs_r, ga_s, ga_r,
    x_s, x_r, wp_s, wp_r, w_s, w_r, z_s, z_r, wa_s, wa_r, wz_s, wz_r,
):
    g, r = lax.axis_index("grp"), lax.axis_index("rsp")
    core, at = r % 2, r // 2
    mate = at * 2 + 1 - core
    gx, gz = g // 2, g % 2
    z_mate = gx * 2 + 1 - gz
    mine = core * PEERS + at

    places = [(at + j) % PEERS for j in range(PEERS)]
    groups = [(g + j) % GRPS for j in range(GRPS)]
    xs = [(gx + j) % NX for j in range(NX)]

    def remote(src, dst, send, recv, grp, rsp):
        return pltpu.make_async_remote_copy(
            src_ref=src, dst_ref=dst, send_sem=send, recv_sem=recv,
            device_id=(grp, rsp), device_id_type=MESH,
        )

    def each(count, f):
        for j in range(1, count):
            f(j)

    loads = [
        pltpu.make_async_copy(src, dst, in_sem.at[n])
        for n, (src, dst) in enumerate(((x_hbm, x), (q_hbm, q), (d_hbm, d), (kv_hbm, own)))
    ]

    def w_loads(h):
        return [
            pltpu.make_async_copy(
                w_hbm.at[:, pl.ds(t * 512 + h * D, D)], w.at[h, :, pl.ds(t * D, D)], w_sem.at[h, t]
            )
            for t in range(2)
        ]

    barrier = pltpu.get_barrier_semaphore()
    each(16, lambda j: pl.semaphore_signal(
        barrier, inc=1, device_id=(g, (r + j) % 16), device_id_type=MESH))
    each(GRPS, lambda j: pl.semaphore_signal(
        barrier, inc=1, device_id=((g + j) % GRPS, r), device_id_type=MESH))

    loads[0].start()
    for h in range(HEADS):
        for c in w_loads(h):
            c.start()
        if h == 1:
            for c in loads[1:]:
                c.start()

    def kv_copy(h, j):
        slot = kv.at[h, mine]
        return remote(slot, slot, kv_s.at[h], kv_r.at[h], g, places[j] * 2 + core)

    def kv_all(h):
        part = kv.at[h, pl.ds(core * PEERS, PEERS - 1)]
        return remote(part, part, kv_s.at[h], kv_r.at[h], g, mate)

    def kv_mate(h, side):
        half = kv.at[h, pl.ds(side * PEERS, PEERS)]
        return remote(half, half, kvp_s.at[h], kvp_r.at[h], g, mate)

    def p_copy(h):
        return remote(pb.at[h, pl.ds((1 - core) * PEERS, PEERS)], pr.at[h], p_s.at[h], p_r.at[h], g, mate)

    def rs_copy(h, j):
        return remote(pb.at[h, core * PEERS + places[j]], rsr.at[h, at], rs_s.at[h], rs_r.at[h],
                      g, places[j] * 2 + core)

    def rs_all(h):
        return remote(pb.at[h, pl.ds(core * PEERS, PEERS - 1)], rsr.at[h, pl.ds(0, PEERS - 1)],
                      rs_s.at[h], rs_r.at[h], g, mate)

    def ga_copy(h, j):
        return remote(ga.at[h, at], ga.at[h, at], ga_s.at[h], ga_r.at[h], g, places[j] * 2 + core)

    def ga_all(h):
        part = ga.at[h, pl.ds(0, PEERS - 1)]
        return remote(part, part, ga_s.at[h], ga_r.at[h], g, mate)

    def x_cols(place):
        return lanes(place * 2 * WROWS, 2 * WROWS)

    def x_copy(j):
        return remote(x.at[:, x_cols(places[j])], xr.at[at], x_s.at[0], x_r.at[0],
                      g, places[j] * 2 + core)

    def x_all():
        part = xr.at[pl.ds(0, PEERS - 1)]
        return remote(part, part, x_s.at[0], x_r.at[0], g, mate)

    def wp_copy(h):
        return remote(wf.at[h], wp.at[h], wp_s.at[h], wp_r.at[h], g, mate)

    def w_copy(h, j):
        return remote(ws.at[h, xs[j]], wr.at[h, gx], w_s.at[h], w_r.at[h], xs[j] * 2 + gz, r)

    def w_all(h):
        return remote(ws.at[h, pl.ds(0, NX - 1)], wr.at[h, pl.ds(0, NX - 1)], w_s.at[h], w_r.at[h], z_mate, r)

    def z_copy(h):
        return remote(zs.at[h], zr.at[h], z_s.at[h], z_r.at[h], z_mate, r)

    def wa_copy(h, j):
        return remote(wa.at[h, gx], wa.at[h, gx], wa_s.at[h], wa_r.at[h], xs[j] * 2 + gz, r)

    def wa_all(h):
        part = wa.at[h, pl.ds(0, NX - 1)]
        return remote(part, part, wa_s.at[h], wa_r.at[h], z_mate, r)

    def wz_copy(j):
        return remote(wz.at[g], wz.at[g], wz_s.at[0], wz_r.at[0], groups[j], r)

    def wz_all():
        part = wz.at[pl.ds(0, GRPS - 1)]
        return remote(part, part, wz_s.at[0], wz_r.at[0], z_mate, r)

    def kv_send(h):
        each(PEERS, lambda j: kv_copy(h, j).start())

    def kv_relay(h):
        kv_all(h).wait_recv()
        kv_mate(h, core).start()

    def project(h):
        for c in w_loads(h):
            c.wait()
        kv[h, mine] = dot(x[...], w[h], NN).astype(BF)

    loads[0].wait()
    project(0)
    pl.semaphore_wait(barrier, 15 + GRPS - 1)
    kv_send(0)
    project(1)

    for c in loads[1:]:
        c.wait()
    row = lax.broadcasted_iota(jnp.int32, (SEQ, D), 0)
    for n in range(2):
        live = jnp.broadcast_to(mask_ref[n:n + 1, :].astype(F32), (SEQ, SEQ)).T
        live = (live == 1.0) & (row < len_ref[n])
        rows = slice(n * SEQ, (n + 1) * SEQ)

        def clear(c, _, rows=rows, live=live):
            cols = lanes(c * D)
            d[rows, cols] = jnp.where(live, d[rows, cols].astype(F32), 0.0).astype(BF)
            return _

        lax.fori_loop(0, HEADS * PER, clear, 0)
    xr[at] = x[:, x_cols(at)]
    xacc[...] = jnp.zeros_like(xacc)

    kv_relay(0)
    kv_send(1)
    project(2)
    project(3)

    causal = (lax.broadcasted_iota(jnp.int32, (ROWS, SEQ), 1)
              <= lax.broadcasted_iota(jnp.int32, (ROWS, SEQ), 0) % SEQ)

    def own_kv(h, n):
        rows = slice(n * SEQ, (n + 1) * SEQ)
        return own[rows, lanes(h * D)], own[rows, lanes(512 + h * D)]

    def kept(h, n):
        return (h % KEPT) * 2 + n

    def softmax_part(h, n):
        rows = slice(n * SEQ, (n + 1) * SEQ)
        qn = jnp.concatenate([q[rows, lanes((h * PER + t) * D)] for t in range(PER)], 0)
        dn = jnp.concatenate([d[rows, lanes((h * PER + t) * D)] for t in range(PER)], 0)
        keys = kv[h, :, :, 0:D].reshape(PROMPT, D)
        values = kv[h, :, :, D:].reshape(PROMPT, D)
        ko, vo = own_kv(h, n)
        none = jnp.zeros_like(ko)
        both = jnp.concatenate(
            [jnp.concatenate([ko, none], 1), jnp.concatenate([none, vo], 1)], 0)
        last = dot(jnp.concatenate([qn, dn], 1), both, NT)
        scores = jnp.concatenate(
            [dot(qn, keys, NT), jnp.where(causal, last[:, :SEQ], -1e30)], 1)
        pgrad = jnp.concatenate([dot(dn, values, NT), last[:, SEQ:]], 1)
        top = jnp.max(scores, axis=1, keepdims=True)
        e = jnp.exp2((scores - top) * (SCALE * LOG2E))
        inv = 1.0 / jnp.sum(e, axis=1, keepdims=True)
        center = jnp.sum(e * pgrad, axis=1, keepdims=True) * inv
        es[n] = e.astype(BF)
        ss[kept(h, n)] = (e * ((pgrad - center) * inv)).astype(BF)
        dd[n] = (dn * inv).astype(BF)

    def key_part(h):
        total = []
        for n in range(2):
            rows = slice(n * SEQ, (n + 1) * SEQ)
            qn = jnp.concatenate([q[rows, lanes((h * PER + t) * D)] for t in range(PER)], 0)
            dk = dot(qn, ss[kept(h, n)], TN) * SCALE
            dv = dot(dd[n], es[n], TN)
            own_g[rows, lanes(h * D)] = dk[:, PROMPT:].astype(BF).T
            own_g[rows, lanes(512 + h * D)] = dv[:, PROMPT:].astype(BF).T
            total.append((dk[:, :PROMPT], dv[:, :PROMPT]))
        dk, dv = total[0][0] + total[1][0], total[0][1] + total[1][1]
        pb[h, :, :, 0:D] = dk.astype(BF).T.reshape(16, TOK, D)
        pb[h, :, :, D:] = dv.astype(BF).T.reshape(16, TOK, D)

    def qg_out(h, n):
        part = (pl.ds(n * SEQ, SEQ), lanes(h * PER * D, PER * D))
        return pltpu.make_async_copy(q.at[part], qg_hbm.at[part], qg_sem.at[h, n])

    def query_part(h, n):
        rows = slice(n * SEQ, (n + 1) * SEQ)
        keys = jnp.concatenate([kv[h, :, :, 0:D].reshape(PROMPT, D), own_kv(h, n)[0]], 0)
        out = (dot(ss[kept(h, n)], keys, NN) * SCALE).astype(BF)
        for t in range(PER):
            q[rows, lanes((h * PER + t) * D)] = out[t * SEQ:(t + 1) * SEQ]
        qg_out(h, n).start()

    def pair_sum(h):
        p_copy(h).wait_recv()
        half = pb[h, pl.ds(core * PEERS, PEERS)].astype(F32) + pr[h].astype(F32)
        pb[h, pl.ds(core * PEERS, PEERS)] = half.astype(BF)
        each(PEERS, lambda j: rs_copy(h, j).start())
        rsr[h, at] = pb[h, mine]

    def group_sum(h):
        rs_all(h).wait_recv()
        total = rsr[h, 0].astype(F32)
        for j in range(1, PEERS):
            total += rsr[h, j].astype(F32)
        ga[h, at] = total.astype(BF)
        each(PEERS, lambda j: ga_copy(h, j).start())

    def x_part(h):
        def tile(c, _):
            rows = pl.ds(c * 1024, 1024)
            xacc[:, lanes(c * 1024, 1024)] += dot(ga[h, at], w[h, rows, :], NT)
            return _

        lax.fori_loop(0, WIDTH // 1024, tile, 0)

    def w_part(h):
        ga_all(h).wait_recv()
        part = dot(xr[...].reshape(PEERS * TOK, 2 * WROWS), ga[h].reshape(PEERS * TOK, 2 * D), TN)
        low, high = part[:WROWS], part[WROWS:]
        wf[h] = jnp.where(core == 0, high, low)
        wo[...] = jnp.where(core == 0, low, high)
        wp_copy(h).start()

    def w_pair(h):
        wp_copy(h).wait_recv()
        ws[h] = (wo[...] + wp[h]).astype(BF).reshape(NX, WPART, 2 * D)
        each(NX, lambda j: w_copy(h, j).start())
        wr[h, gx] = ws[h, gx]

    def w_sum(h):
        w_all(h).wait_recv()
        total = wr[h, 0].astype(F32)
        for j in range(1, NX):
            total += wr[h, j].astype(F32)
        zs[h] = total.astype(BF)
        z_copy(h).start()

    def w_sum_last(h):
        w_all(h).wait_recv()
        total = wr[h, 0].astype(F32)
        for j in range(1, NX):
            total += wr[h, j].astype(F32)
        wz[g] = total.astype(BF)
        each(GRPS, lambda j: wz_copy(j).start())

    def w_out_last(h):
        wz_all().wait_recv()
        for i in range(NX):
            wa[h, i] = (wz[2 * i].astype(F32) + wz[2 * i + 1].astype(F32)).astype(BF)
        wa_out(h).start()

    def z_sum(h):
        z_copy(h).wait_recv()
        wa[h, gx] = (zs[h].astype(F32) + zr[h].astype(F32)).astype(BF)
        each(NX, lambda j: wa_copy(h, j).start())

    def wa_out(h):
        return pltpu.make_async_copy(wa.at[h], wa_hbm.at[h], out_sem.at[2 + h])

    def w_out(h):
        wa_all(h).wait_recv()
        wa_out(h).start()

    def when(cond):
        return pl.when(cond) if not isinstance(cond, bool) else (lambda f: f() if cond else None)

    def head(h, c):
        kv_mate(h, 1 - core).wait_recv()
        softmax_part(h, 0)

        @when(h >= 1)
        def _():
            pair_sum(h - 1)

        @when(h < HEADS - 2)
        def _():
            kv_send(h + 2)

        @when(h == HEADS - 1)
        def _():
            w_part(0)

        softmax_part(h, 1)

        @when(h < HEADS - 1)
        def _():
            kv_relay(h + 1)

        @when(h >= 2)
        def _():
            group_sum(h - 2)

        @when(h == HEADS - 1)
        def _():
            w_pair(0)

        key_part(h)
        p_copy(h).start()

        @when(h == 0)
        def _():
            each(PEERS, lambda j: x_copy(j).start())

        @when(h == 2)
        def _():
            x_all().wait_recv()

        @when(h < HEADS - KEPT)
        def _():
            query_part(h, 0)
            query_part(h, 1)

        return c

    lax.fori_loop(0, HEADS, head, 0)

    own_out = pltpu.make_async_copy(own_g, own_hbm, out_sem.at[0])
    xg_out = pltpu.make_async_copy(x, xg_hbm, out_sem.at[1])
    own_out.start()
    query_part(0, 0)
    pair_sum(3)
    group_sum(2)
    query_part(0, 1)
    w_sum(0)
    query_part(1, 0)
    w_part(1)
    query_part(1, 1)
    w_pair(1)
    group_sum(3)
    x_part(0)
    w_part(2)
    z_sum(0)
    query_part(2, 0)
    w_pair(2)
    w_sum(1)
    query_part(2, 1)
    x_part(1)
    w_part(3)
    z_sum(1)
    query_part(3, 0)
    w_pair(3)
    w_sum(2)
    w_out(0)
    query_part(3, 1)
    x_part(2)
    x_part(3)
    w_sum_last(3)
    z_sum(2)
    w_out(1)
    x_all().wait_send()
    x[...] = xacc[...].astype(BF)
    xg_out.start()

    def sent(h, c):
        kv_all(h).wait_send()
        kv_mate(h, core).wait_send()
        p_copy(h).wait_send()
        rs_all(h).wait_send()
        ga_all(h).wait_send()
        wp_copy(h).wait_send()
        w_all(h).wait_send()
        for n in range(2):
            qg_out(h, n).wait()
        return c

    lax.fori_loop(0, HEADS, sent, 0)
    own_out.wait()
    xg_out.wait()
    w_out(2)
    w_out_last(3)

    def gathered(h, c):
        z_copy(h).wait_send()
        wa_all(h).wait_send()
        return c

    lax.fori_loop(0, HEADS - 1, gathered, 0)
    wz_all().wait_send()
    for h in range(HEADS):
        wa_out(h).wait()


CHUNKS = 4


def finish(qg_in, own_in, xg_in, wa_in, qg, own_g, xg, wg, qv, ov, xv, wav, wv, in_sem, out_sem):
    size = 2 * SEQ // CHUNKS
    moves = [(wa_in, wav, None)]
    for i in range(CHUNKS):
        part = pl.ds(i * size, size)
        moves.append((qg_in.at[part], qv.at[part], qg.at[part]))
    moves += [(own_in, ov, own_g), (xg_in, xv, xg)]
    ins = [pltpu.make_async_copy(src, mid, in_sem.at[n]) for n, (src, mid, _) in enumerate(moves)]
    outs = [pltpu.make_async_copy(mid, dst, out_sem.at[n])
            for n, (_, mid, dst) in enumerate(moves) if dst is not None]
    w_out = pltpu.make_async_copy(wv, wg, out_sem.at[0])
    for c in ins:
        c.start()
    ins[0].wait()
    for h in range(HEADS):
        full = wav[h].astype(F32).reshape(WROWS, 2 * D)
        for t in range(2):
            wv[:, t * 512 + h * D:t * 512 + (h + 1) * D] = full[:, t * D:(t + 1) * D]
    w_out.start()
    for c, o in zip(ins[1:], outs):
        c.wait()
        o.start()
    w_out.wait()
    for o in outs:
        o.wait()


def local(prompt_x, key_value_weight, queries, resp_kv, out_grad, lengths, token_mask):
    dma = pltpu.SemaphoreType.DMA
    vmem = pl.BlockSpec(memory_space=pltpu.VMEM)
    hbm = pl.BlockSpec(memory_space=pl.ANY)
    pairs = lambda *shape: [dma(shape), dma(shape)]
    qg_shape = jax.ShapeDtypeStruct((2 * SEQ, HEADS * PER * D), BF)
    own_shape = jax.ShapeDtypeStruct((2 * SEQ, 2 * HEADS * D), BF)
    xg_shape = jax.ShapeDtypeStruct((TOK, WIDTH), BF)
    parts = pl.pallas_call(
        kernel,
        out_shape=(
            qg_shape, own_shape, xg_shape,
            jax.ShapeDtypeStruct((HEADS, NX, WPART, 2 * D), BF),
        ),
        in_specs=[hbm] * 5 + [pl.BlockSpec(memory_space=pltpu.SMEM), vmem],
        out_specs=(hbm,) * 4,
        scratch_shapes=[
            pltpu.VMEM((TOK, WIDTH), BF),
            pltpu.VMEM((HEADS, WIDTH, 2 * D), BF),
            pltpu.VMEM((2 * SEQ, HEADS * PER * D), BF),
            pltpu.VMEM((2 * SEQ, HEADS * PER * D), BF),
            pltpu.VMEM((2 * SEQ, 2 * HEADS * D), BF),
            pltpu.VMEM((2 * SEQ, 2 * HEADS * D), BF),
            pltpu.VMEM((HEADS, 16, TOK, 2 * D), BF),
            pltpu.VMEM((HEADS, 16, TOK, 2 * D), BF),
            pltpu.VMEM((HEADS, PEERS, TOK, 2 * D), BF),
            pltpu.VMEM((HEADS, PEERS, TOK, 2 * D), BF),
            pltpu.VMEM((HEADS, PEERS, TOK, 2 * D), BF),
            pltpu.VMEM((PEERS, TOK, 2 * WROWS), BF),
            pltpu.VMEM((HEADS, WROWS, 2 * D), F32),
            pltpu.VMEM((WROWS, 2 * D), F32),
            pltpu.VMEM((HEADS, WROWS, 2 * D), F32),
            pltpu.VMEM((HEADS, NX, WPART, 2 * D), BF),
            pltpu.VMEM((HEADS, NX, WPART, 2 * D), BF),
            pltpu.VMEM((HEADS, WPART, 2 * D), BF),
            pltpu.VMEM((HEADS, WPART, 2 * D), BF),
            pltpu.VMEM((HEADS, NX, WPART, 2 * D), BF),
            pltpu.VMEM((GRPS, WPART, 2 * D), BF),
            pltpu.VMEM((2, ROWS, KEYS), BF),
            pltpu.VMEM((2 * KEPT, ROWS, KEYS), BF),
            pltpu.VMEM((2, ROWS, D), BF),
            pltpu.VMEM((TOK, WIDTH), F32),
            dma((4,)),
            dma((HEADS, 2)),
            dma((HEADS, 2)),
            dma((2 + HEADS,)),
            *pairs(HEADS),
            *pairs(HEADS),
            *pairs(HEADS),
            *pairs(HEADS),
            *pairs(HEADS),
            *pairs(1),
            *pairs(HEADS),
            *pairs(HEADS),
            *pairs(HEADS),
            *pairs(HEADS),
            *pairs(1),
        ],
        compiler_params=pltpu.CompilerParams(
            collective_id=0, has_side_effects=True, vmem_limit_bytes=64 << 20
        ),
    )(prompt_x, key_value_weight, queries, resp_kv, out_grad, lengths, token_mask)
    return pl.pallas_call(
        finish,
        out_shape=(
            qg_shape, own_shape, xg_shape,
            jax.ShapeDtypeStruct((WROWS, 2 * HEADS * D), F32),
        ),
        in_specs=[hbm] * 4,
        out_specs=(hbm,) * 4,
        scratch_shapes=[
            pltpu.VMEM(qg_shape.shape, BF),
            pltpu.VMEM(own_shape.shape, BF),
            pltpu.VMEM(xg_shape.shape, BF),
            pltpu.VMEM((HEADS, NX, WPART, 2 * D), BF),
            pltpu.VMEM((WROWS, 2 * HEADS * D), F32),
            dma((3 + CHUNKS,)),
            dma((3 + CHUNKS,)),
        ],
        compiler_params=pltpu.CompilerParams(vmem_limit_bytes=60 << 20),
    )(*parts)


def solution(mesh):
    rows = P(("grp", "rsp"), None)
    return jax.shard_map(
        local,
        mesh=mesh,
        in_specs=(rows, P(), rows, rows, rows, P(("grp", "rsp")), rows),
        out_specs=(rows, rows, rows, P("rsp", None)),
        check_vma=False,
    )
```

```python
import functools

import jax
import jax.numpy as jnp
from jax import lax
from jax.experimental import pallas as pl
from jax.experimental.pallas import tpu as pltpu
from jax.sharding import PartitionSpec as P

HEADS = 4
PER = 8
D = 128
SEQ = 128
ROWS = PER * SEQ
PROMPT = 1024
KEYS = PROMPT + SEQ
TOK = 64
WIDTH = 5120
PEERS = 8
WROWS = 320
GRPS = 8
WPART = 80
KEPT = 4
BF = jnp.bfloat16
F32 = jnp.float32
SCALE = D**-0.5
LOG2E = 1.4426950408889634
MESH = pl.DeviceIdType.MESH
NN = ((1,), (0,))
NT = ((1,), (1,))
TN = ((0,), (0,))


def dot(a, b, dims):
    return lax.dot_general(a, b, (dims, ((), ())), preferred_element_type=F32)


def lanes(start, size=D):
    return pl.ds(pl.multiple_of(start, D), size)


def kernel(
    x_hbm, w_hbm, q_hbm, kv_hbm, d_hbm, len_ref, mask_ref,
    qg_hbm, own_hbm, xg_hbm, wa_hbm,
    x, w, q, d, own, own_g,
    kv, pb, pr, rsr, ga, xr, wf, wo, wp, ws, wr, wa,
    es, ss, dd, xacc,
    in_sem, w_sem, qg_sem, out_sem,
    kv_s, kv_r, kvp_s, kvp_r, p_s, p_r, rs_s, rs_r, ga_s, ga_r,
    x_s, x_r, wp_s, wp_r, w_s, w_r, wa_s, wa_r,
):
    g, r = lax.axis_index("grp"), lax.axis_index("rsp")
    core, at = r % 2, r // 2
    mate = at * 2 + 1 - core
    mine = core * PEERS + at

    places = [(at + j) % PEERS for j in range(PEERS)]
    groups = [(g + j) % GRPS for j in range(GRPS)]

    def remote(src, dst, send, recv, grp, rsp):
        return pltpu.make_async_remote_copy(
            src_ref=src, dst_ref=dst, send_sem=send, recv_sem=recv,
            device_id=(grp, rsp), device_id_type=MESH,
        )

    def each(count, f):
        for j in range(1, count):
            f(j)

    loads = [
        pltpu.make_async_copy(src, dst, in_sem.at[n])
        for n, (src, dst) in enumerate(((x_hbm, x), (q_hbm, q), (d_hbm, d), (kv_hbm, own)))
    ]

    def w_loads(h):
        return [
            pltpu.make_async_copy(
                w_hbm.at[:, pl.ds(t * 512 + h * D, D)], w.at[h, :, pl.ds(t * D, D)], w_sem.at[h, t]
            )
            for t in range(2)
        ]

    barrier = pltpu.get_barrier_semaphore()
    each(16, lambda j: pl.semaphore_signal(
        barrier, inc=1, device_id=(g, (r + j) % 16), device_id_type=MESH))
    each(GRPS, lambda j: pl.semaphore_signal(
        barrier, inc=1, device_id=((g + j) % GRPS, r), device_id_type=MESH))

    loads[0].start()
    for h in range(HEADS):
        for c in w_loads(h):
            c.start()
        if h == 1:
            for c in loads[1:]:
                c.start()

    def kv_copy(h, n, j):
        part = (pl.ds(h, n), mine)
        return remote(kv.at[part], kv.at[part], kv_s.at[h], kv_r.at[h], g, places[j] * 2 + core)

    def kv_all(h, n):
        part = (pl.ds(h, n), pl.ds(core * PEERS, PEERS - 1))
        return remote(kv.at[part], kv.at[part], kv_s.at[h], kv_r.at[h], g, mate)

    def kv_mate(h, n, side):
        part = (pl.ds(h, n), pl.ds(side * PEERS, PEERS))
        return remote(kv.at[part], kv.at[part], kvp_s.at[h], kvp_r.at[h], g, mate)

    def p_copy(h):
        return remote(pb.at[h, pl.ds((1 - core) * PEERS, PEERS)], pr.at[h], p_s.at[h], p_r.at[h], g, mate)

    def rs_copy(h, j):
        return remote(pb.at[h, core * PEERS + places[j]], rsr.at[h, at], rs_s.at[h], rs_r.at[h],
                      g, places[j] * 2 + core)

    def rs_all(h):
        return remote(pb.at[h, pl.ds(core * PEERS, PEERS - 1)], rsr.at[h, pl.ds(0, PEERS - 1)],
                      rs_s.at[h], rs_r.at[h], g, mate)

    def ga_copy(h, j):
        return remote(ga.at[h, at], ga.at[h, at], ga_s.at[h], ga_r.at[h], g, places[j] * 2 + core)

    def ga_all(h):
        part = ga.at[h, pl.ds(0, PEERS - 1)]
        return remote(part, part, ga_s.at[h], ga_r.at[h], g, mate)

    def x_cols(place):
        return lanes(place * 2 * WROWS, 2 * WROWS)

    def x_copy(j):
        return remote(x.at[:, x_cols(places[j])], xr.at[at], x_s.at[0], x_r.at[0],
                      g, places[j] * 2 + core)

    def x_all():
        part = xr.at[pl.ds(0, PEERS - 1)]
        return remote(part, part, x_s.at[0], x_r.at[0], g, mate)

    def wp_copy(h, n):
        part = pl.ds(h, n)
        return remote(wf.at[part], wp.at[part], wp_s.at[h], wp_r.at[h], g, mate)

    def w_copy(h, n, j):
        part = pl.ds(h, n)
        return remote(ws.at[part, groups[j]], wr.at[part, g], w_s.at[h], w_r.at[h], groups[j], r)

    def w_all(h, n):
        part = (pl.ds(h, n), pl.ds(0, GRPS - 1))
        return remote(ws.at[part], wr.at[part], w_s.at[h], w_r.at[h], groups[1], r)

    def wa_copy(h, n, j):
        part = (pl.ds(h, n), g)
        return remote(wa.at[part], wa.at[part], wa_s.at[h], wa_r.at[h], groups[j], r)

    def wa_all(h, n):
        part = (pl.ds(h, n), pl.ds(0, GRPS - 1))
        return remote(wa.at[part], wa.at[part], wa_s.at[h], wa_r.at[h], groups[1], r)

    def kv_send(h, n):
        each(PEERS, lambda j: kv_copy(h, n, j).start())

    def kv_relay(h, n):
        kv_all(h, n).wait_recv()
        kv_mate(h, n, core).start()

    def project(h):
        for c in w_loads(h):
            c.wait()
        kv[h, mine] = dot(x[...], w[h], NN).astype(BF)

    loads[0].wait()
    project(0)
    pl.semaphore_wait(barrier, 15 + GRPS - 1)
    kv_send(0, 1)
    project(1)

    for c in loads[1:]:
        c.wait()
    row = lax.broadcasted_iota(jnp.int32, (SEQ, D), 0)
    for n in range(2):
        live = jnp.broadcast_to(mask_ref[n:n + 1, :].astype(F32), (SEQ, SEQ)).T
        live = (live == 1.0) & (row < len_ref[n])
        rows = slice(n * SEQ, (n + 1) * SEQ)

        def clear(c, _, rows=rows, live=live):
            cols = lanes(c * D)
            d[rows, cols] = jnp.where(live, d[rows, cols].astype(F32), 0.0).astype(BF)
            return _

        lax.fori_loop(0, HEADS * PER, clear, 0)
    xr[at] = x[:, x_cols(at)]
    xacc[...] = jnp.zeros_like(xacc)

    kv_relay(0, 1)
    kv_send(1, 1)
    project(2)
    project(3)

    causal = (lax.broadcasted_iota(jnp.int32, (ROWS, SEQ), 1)
              <= lax.broadcasted_iota(jnp.int32, (ROWS, SEQ), 0) % SEQ)

    def own_kv(h, n):
        rows = slice(n * SEQ, (n + 1) * SEQ)
        return own[rows, lanes(h * D)], own[rows, lanes(512 + h * D)]

    def kept(h, n):
        return (h % KEPT) * 2 + n

    def softmax_part(h, n):
        rows = slice(n * SEQ, (n + 1) * SEQ)
        qn = jnp.concatenate([q[rows, lanes((h * PER + t) * D)] for t in range(PER)], 0)
        dn = jnp.concatenate([d[rows, lanes((h * PER + t) * D)] for t in range(PER)], 0)
        keys = kv[h, :, :, 0:D].reshape(PROMPT, D)
        values = kv[h, :, :, D:].reshape(PROMPT, D)
        ko, vo = own_kv(h, n)
        none = jnp.zeros_like(ko)
        both = jnp.concatenate(
            [jnp.concatenate([ko, none], 1), jnp.concatenate([none, vo], 1)], 0)
        last = dot(jnp.concatenate([qn, dn], 1), both, NT)
        scores = jnp.concatenate(
            [dot(qn, keys, NT), jnp.where(causal, last[:, :SEQ], -1e30)], 1)
        pgrad = jnp.concatenate([dot(dn, values, NT), last[:, SEQ:]], 1)
        top = jnp.max(scores, axis=1, keepdims=True)
        e = jnp.exp2((scores - top) * (SCALE * LOG2E))
        inv = 1.0 / jnp.sum(e, axis=1, keepdims=True)
        center = jnp.sum(e * pgrad, axis=1, keepdims=True) * inv
        es[n] = e.astype(BF)
        ss[kept(h, n)] = (e * ((pgrad - center) * inv)).astype(BF)
        dd[n] = (dn * inv).astype(BF)

    def key_part(h):
        total = []
        for n in range(2):
            rows = slice(n * SEQ, (n + 1) * SEQ)
            qn = jnp.concatenate([q[rows, lanes((h * PER + t) * D)] for t in range(PER)], 0)
            dk = dot(qn, ss[kept(h, n)], TN) * SCALE
            dv = dot(dd[n], es[n], TN)
            own_g[rows, lanes(h * D)] = dk[:, PROMPT:].astype(BF).T
            own_g[rows, lanes(512 + h * D)] = dv[:, PROMPT:].astype(BF).T
            total.append((dk[:, :PROMPT], dv[:, :PROMPT]))
        dk, dv = total[0][0] + total[1][0], total[0][1] + total[1][1]
        pb[h, :, :, 0:D] = dk.astype(BF).T.reshape(16, TOK, D)
        pb[h, :, :, D:] = dv.astype(BF).T.reshape(16, TOK, D)

    def qg_out(h, n):
        part = (pl.ds(n * SEQ, SEQ), lanes(h * PER * D, PER * D))
        return pltpu.make_async_copy(q.at[part], qg_hbm.at[part], qg_sem.at[h, n])

    def query_part(h, n):
        rows = slice(n * SEQ, (n + 1) * SEQ)
        keys = jnp.concatenate([kv[h, :, :, 0:D].reshape(PROMPT, D), own_kv(h, n)[0]], 0)
        out = (dot(ss[kept(h, n)], keys, NN) * SCALE).astype(BF)
        for t in range(PER):
            q[rows, lanes((h * PER + t) * D)] = out[t * SEQ:(t + 1) * SEQ]
        qg_out(h, n).start()

    def pair_sum(h):
        p_copy(h).wait_recv()
        half = pb[h, pl.ds(core * PEERS, PEERS)].astype(F32) + pr[h].astype(F32)
        pb[h, pl.ds(core * PEERS, PEERS)] = half.astype(BF)
        each(PEERS, lambda j: rs_copy(h, j).start())
        rsr[h, at] = pb[h, mine]

    def group_sum(h):
        rs_all(h).wait_recv()
        total = rsr[h, 0].astype(F32)
        for j in range(1, PEERS):
            total += rsr[h, j].astype(F32)
        ga[h, at] = total.astype(BF)
        each(PEERS, lambda j: ga_copy(h, j).start())

    def x_part(h):
        def tile(c, _):
            rows = pl.ds(c * 1024, 1024)
            xacc[:, lanes(c * 1024, 1024)] += dot(ga[h, at], w[h, rows, :], NT)
            return _

        lax.fori_loop(0, WIDTH // 1024, tile, 0)

    def w_part(h):
        part = dot(xr[...].reshape(PEERS * TOK, 2 * WROWS), ga[h].reshape(PEERS * TOK, 2 * D), TN)
        low, high = part[:WROWS], part[WROWS:]
        wf[h] = jnp.where(core == 0, high, low).astype(BF)
        wo[h % 2] = jnp.where(core == 0, low, high)

    def w_send(h, n):
        for i in range(h, h + n):
            ga_all(i).wait_recv()
            w_part(i)
        wp_copy(h, n).start()

    def w_pair(h, n):
        wp_copy(h, n).wait_recv()
        for k in range(h, h + n):
            part = (wo[k % 2] + wp[k].astype(F32)).astype(BF)
            for i in range(4):
                for t in range(2):
                    ws[k, i * 2 + t] = part[i * WPART:(i + 1) * WPART, t * D:(t + 1) * D]
        each(GRPS, lambda j: w_copy(h, n, j).start())
        for k in range(h, h + n):
            wr[k, g] = ws[k, g]

    def w_sum(h, n):
        w_all(h, n).wait_recv()
        for k in range(h, h + n):
            total = wr[k, 0].astype(F32)
            for j in range(1, GRPS):
                total += wr[k, j].astype(F32)
            wa[k, g] = total.astype(BF)
        each(GRPS, lambda j: wa_copy(h, n, j).start())

    def wa_out(h, n):
        part = pl.ds(h, n)
        return pltpu.make_async_copy(wa.at[part], wa_hbm.at[part], out_sem.at[2 + h])

    def w_out(h, n):
        wa_all(h, n).wait_recv()
        wa_out(h, n).start()

    def when(cond):
        return pl.when(cond) if not isinstance(cond, bool) else (lambda f: f() if cond else None)

    def head(h, c):
        @when(h < 2)
        def _():
            kv_mate(h, 1, 1 - core).wait_recv()

        @when(h == 2)
        def _():
            kv_mate(2, 2, 1 - core).wait_recv()

        softmax_part(h, 0)

        @when(h >= 1)
        def _():
            pair_sum(h - 1)

        @when(h == 0)
        def _():
            kv_send(2, 2)

        softmax_part(h, 1)

        @when(h == 0)
        def _():
            kv_relay(1, 1)

        @when(h == 1)
        def _():
            kv_relay(2, 2)

        @when(h >= 2)
        def _():
            group_sum(h - 2)

        key_part(h)
        p_copy(h).start()

        @when(h == 0)
        def _():
            each(PEERS, lambda j: x_copy(j).start())

        return c

    lax.fori_loop(0, HEADS, head, 0)

    own_out = pltpu.make_async_copy(own_g, own_hbm, out_sem.at[0])
    xg_out = pltpu.make_async_copy(x, xg_hbm, out_sem.at[1])
    own_out.start()
    query_part(0, 0)
    pair_sum(3)
    group_sum(2)
    query_part(0, 1)
    x_all().wait_recv()
    w_send(0, 2)
    query_part(1, 0)
    w_pair(0, 2)
    group_sum(3)
    x_part(0)
    query_part(1, 1)
    w_send(2, 1)
    x_part(1)
    w_pair(2, 1)
    query_part(2, 0)
    query_part(2, 1)
    w_send(3, 1)
    w_sum(0, 2)
    x_part(2)
    w_pair(3, 1)
    w_sum(2, 1)
    query_part(3, 0)
    query_part(3, 1)
    x_part(3)
    x_all().wait_send()
    x[...] = xacc[...].astype(BF)
    xg_out.start()
    w_sum(3, 1)
    w_out(0, 2)

    for h in range(HEADS):
        p_copy(h).wait_send()
        rs_all(h).wait_send()
        ga_all(h).wait_send()
        for n in range(2):
            qg_out(h, n).wait()
    for h, n in ((0, 1), (1, 1), (2, 2)):
        kv_all(h, n).wait_send()
        kv_mate(h, n, core).wait_send()
    own_out.wait()
    w_out(2, 1)
    for h, n in ((0, 2), (2, 1), (3, 1)):
        wp_copy(h, n).wait_send()
        w_all(h, n).wait_send()
    xg_out.wait()
    w_out(3, 1)
    for h, n in ((0, 2), (2, 1), (3, 1)):
        wa_all(h, n).wait_send()
        wa_out(h, n).wait()


CHUNKS = 4


def finish(qg_in, own_in, xg_in, wa_in, qg, own_g, xg, wg, qv, ov, xv, wav, wv, in_sem, out_sem):
    size = 2 * SEQ // CHUNKS
    moves = [(wa_in, wav, None)]
    for i in range(CHUNKS):
        part = pl.ds(i * size, size)
        moves.append((qg_in.at[part], qv.at[part], qg.at[part]))
    moves += [(own_in, ov, own_g), (xg_in, xv, xg)]
    ins = [pltpu.make_async_copy(src, mid, in_sem.at[n]) for n, (src, mid, _) in enumerate(moves)]
    outs = [pltpu.make_async_copy(mid, dst, out_sem.at[n])
            for n, (_, mid, dst) in enumerate(moves) if dst is not None]
    w_out = pltpu.make_async_copy(wv, wg, out_sem.at[0])
    for c in ins:
        c.start()
    ins[0].wait()
    for h in range(HEADS):
        for i in range(4):
            for t in range(2):
                wv[i * WPART:(i + 1) * WPART, t * 512 + h * D:t * 512 + (h + 1) * D] = (
                    wav[h, i * 2 + t].astype(F32))
    w_out.start()
    for c, o in zip(ins[1:], outs):
        c.wait()
        o.start()
    w_out.wait()
    for o in outs:
        o.wait()


def local(prompt_x, key_value_weight, queries, resp_kv, out_grad, lengths, token_mask):
    dma = pltpu.SemaphoreType.DMA
    vmem = pl.BlockSpec(memory_space=pltpu.VMEM)
    hbm = pl.BlockSpec(memory_space=pl.ANY)
    pairs = lambda *shape: [dma(shape), dma(shape)]
    qg_shape = jax.ShapeDtypeStruct((2 * SEQ, HEADS * PER * D), BF)
    own_shape = jax.ShapeDtypeStruct((2 * SEQ, 2 * HEADS * D), BF)
    xg_shape = jax.ShapeDtypeStruct((TOK, WIDTH), BF)
    parts = pl.pallas_call(
        kernel,
        out_shape=(
            qg_shape, own_shape, xg_shape,
            jax.ShapeDtypeStruct((HEADS, GRPS, WPART, D), BF),
        ),
        in_specs=[hbm] * 5 + [pl.BlockSpec(memory_space=pltpu.SMEM), vmem],
        out_specs=(hbm,) * 4,
        scratch_shapes=[
            pltpu.VMEM((TOK, WIDTH), BF),
            pltpu.VMEM((HEADS, WIDTH, 2 * D), BF),
            pltpu.VMEM((2 * SEQ, HEADS * PER * D), BF),
            pltpu.VMEM((2 * SEQ, HEADS * PER * D), BF),
            pltpu.VMEM((2 * SEQ, 2 * HEADS * D), BF),
            pltpu.VMEM((2 * SEQ, 2 * HEADS * D), BF),
            pltpu.VMEM((HEADS, 16, TOK, 2 * D), BF),
            pltpu.VMEM((HEADS, 16, TOK, 2 * D), BF),
            pltpu.VMEM((HEADS, PEERS, TOK, 2 * D), BF),
            pltpu.VMEM((HEADS, PEERS, TOK, 2 * D), BF),
            pltpu.VMEM((HEADS, PEERS, TOK, 2 * D), BF),
            pltpu.VMEM((PEERS, TOK, 2 * WROWS), BF),
            pltpu.VMEM((HEADS, WROWS, 2 * D), BF),
            pltpu.VMEM((2, WROWS, 2 * D), F32),
            pltpu.VMEM((HEADS, WROWS, 2 * D), BF),
            pltpu.VMEM((HEADS, GRPS, WPART, D), BF),
            pltpu.VMEM((HEADS, GRPS, WPART, D), BF),
            pltpu.VMEM((HEADS, GRPS, WPART, D), BF),
            pltpu.VMEM((2, ROWS, KEYS), BF),
            pltpu.VMEM((2 * KEPT, ROWS, KEYS), BF),
            pltpu.VMEM((2, ROWS, D), BF),
            pltpu.VMEM((TOK, WIDTH), F32),
            dma((4,)),
            dma((HEADS, 2)),
            dma((HEADS, 2)),
            dma((2 + HEADS,)),
            *pairs(HEADS),
            *pairs(HEADS),
            *pairs(HEADS),
            *pairs(HEADS),
            *pairs(HEADS),
            *pairs(1),
            *pairs(HEADS),
            *pairs(HEADS),
            *pairs(HEADS),
        ],
        compiler_params=pltpu.CompilerParams(
            collective_id=0, has_side_effects=True, vmem_limit_bytes=64 << 20
        ),
    )(prompt_x, key_value_weight, queries, resp_kv, out_grad, lengths, token_mask)
    return pl.pallas_call(
        finish,
        out_shape=(
            qg_shape, own_shape, xg_shape,
            jax.ShapeDtypeStruct((WROWS, 2 * HEADS * D), F32),
        ),
        in_specs=[hbm] * 4,
        out_specs=(hbm,) * 4,
        scratch_shapes=[
            pltpu.VMEM(qg_shape.shape, BF),
            pltpu.VMEM(own_shape.shape, BF),
            pltpu.VMEM(xg_shape.shape, BF),
            pltpu.VMEM((HEADS, GRPS, WPART, D), BF),
            pltpu.VMEM((WROWS, 2 * HEADS * D), F32),
            dma((3 + CHUNKS,)),
            dma((3 + CHUNKS,)),
        ],
        compiler_params=pltpu.CompilerParams(vmem_limit_bytes=60 << 20),
    )(*parts)


def solution(mesh):
    rows = P(("grp", "rsp"), None)
    return jax.shard_map(
        local,
        mesh=mesh,
        in_specs=(rows, P(), rows, rows, rows, P(("grp", "rsp")), rows),
        out_specs=(rows, rows, rows, P("rsp", None)),
        check_vma=False,
    )
```

```python
import functools

import jax
import jax.numpy as jnp
from jax import lax
from jax.experimental import pallas as pl
from jax.experimental.pallas import tpu as pltpu
from jax.sharding import PartitionSpec as P

HEADS = 4
PER = 8
D = 128
SEQ = 128
ROWS = PER * SEQ
PROMPT = 1024
KEYS = PROMPT + SEQ
TOK = 64
WIDTH = 5120
PEERS = 8
WROWS = 320
GRPS = 8
WPART = 80
KEPT = 4
BF = jnp.bfloat16
F32 = jnp.float32
SCALE = D**-0.5
LOG2E = 1.4426950408889634
MESH = pl.DeviceIdType.MESH
NN = ((1,), (0,))
NT = ((1,), (1,))
TN = ((0,), (0,))


def dot(a, b, dims):
    return lax.dot_general(a, b, (dims, ((), ())), preferred_element_type=F32)


def lanes(start, size=D):
    return pl.ds(pl.multiple_of(start, D), size)


def kernel(
    x_hbm, w_hbm, q_hbm, kv_hbm, d_hbm, len_ref, mask_ref,
    qg_hbm, own_hbm, xg_hbm, wa_hbm,
    x, w, q, d, own, own_g,
    kv, pb, pr, rsr, ga, xr, wf, wo, wp, ws, wr, wa,
    es, ss, dd, xacc,
    in_sem, w_sem, qg_sem, out_sem,
    kv_s, kv_r, kvp_s, kvp_r, p_s, p_r, rs_s, rs_r, ga_s, ga_r,
    x_s, x_r, wp_s, wp_r, w_s, w_r, wa_s, wa_r,
):
    g, r = lax.axis_index("grp"), lax.axis_index("rsp")
    core, at = r % 2, r // 2
    mate = at * 2 + 1 - core
    mine = core * PEERS + at

    places = [(at + j) % PEERS for j in range(PEERS)]
    groups = [(g + j) % GRPS for j in range(GRPS)]

    def remote(src, dst, send, recv, grp, rsp):
        return pltpu.make_async_remote_copy(
            src_ref=src, dst_ref=dst, send_sem=send, recv_sem=recv,
            device_id=(grp, rsp), device_id_type=MESH,
        )

    def each(count, f):
        for j in range(1, count):
            f(j)

    loads = [
        pltpu.make_async_copy(src, dst, in_sem.at[n])
        for n, (src, dst) in enumerate(((x_hbm, x), (q_hbm, q), (d_hbm, d), (kv_hbm, own)))
    ]

    def w_loads(h):
        return [
            pltpu.make_async_copy(
                w_hbm.at[:, pl.ds(t * 512 + h * D, D)], w.at[h, :, pl.ds(t * D, D)], w_sem.at[h, t]
            )
            for t in range(2)
        ]

    barrier = pltpu.get_barrier_semaphore()
    each(16, lambda j: pl.semaphore_signal(
        barrier, inc=1, device_id=(g, (r + j) % 16), device_id_type=MESH))
    each(GRPS, lambda j: pl.semaphore_signal(
        barrier, inc=1, device_id=((g + j) % GRPS, r), device_id_type=MESH))

    loads[0].start()
    for h in range(HEADS):
        for c in w_loads(h):
            c.start()
        if h == 1:
            for c in loads[1:]:
                c.start()

    def kv_copy(h, n, j):
        part = (pl.ds(h, n), mine)
        return remote(kv.at[part], kv.at[part], kv_s.at[h], kv_r.at[h], g, places[j] * 2 + core)

    def kv_all(h, n):
        part = (pl.ds(h, n), pl.ds(core * PEERS, PEERS - 1))
        return remote(kv.at[part], kv.at[part], kv_s.at[h], kv_r.at[h], g, mate)

    def kv_mate(h, n, side):
        part = (pl.ds(h, n), pl.ds(side * PEERS, PEERS))
        return remote(kv.at[part], kv.at[part], kvp_s.at[h], kvp_r.at[h], g, mate)

    def p_copy(h):
        return remote(pb.at[h, pl.ds((1 - core) * PEERS, PEERS)], pr.at[h], p_s.at[h], p_r.at[h], g, mate)

    def rs_copy(h, j):
        return remote(pb.at[h, core * PEERS + places[j]], rsr.at[h, at], rs_s.at[h], rs_r.at[h],
                      g, places[j] * 2 + core)

    def rs_all(h):
        return remote(pb.at[h, pl.ds(core * PEERS, PEERS - 1)], rsr.at[h, pl.ds(0, PEERS - 1)],
                      rs_s.at[h], rs_r.at[h], g, mate)

    def ga_copy(h, j):
        return remote(ga.at[h, at], ga.at[h, at], ga_s.at[h], ga_r.at[h], g, places[j] * 2 + core)

    def ga_all(h):
        part = ga.at[h, pl.ds(0, PEERS - 1)]
        return remote(part, part, ga_s.at[h], ga_r.at[h], g, mate)

    def x_cols(place):
        return lanes(place * 2 * WROWS, 2 * WROWS)

    def x_copy(j):
        return remote(x.at[:, x_cols(places[j])], xr.at[at], x_s.at[0], x_r.at[0],
                      g, places[j] * 2 + core)

    def x_all():
        part = xr.at[pl.ds(0, PEERS - 1)]
        return remote(part, part, x_s.at[0], x_r.at[0], g, mate)

    def wp_copy(h, n):
        part = pl.ds(h, n)
        return remote(wf.at[part], wp.at[part], wp_s.at[h], wp_r.at[h], g, mate)

    def w_copy(h, n, j):
        part = pl.ds(h, n)
        return remote(ws.at[part, groups[j]], wr.at[part, g], w_s.at[h], w_r.at[h], groups[j], r)

    def w_all(h, n):
        part = (pl.ds(h, n), pl.ds(0, GRPS - 1))
        return remote(ws.at[part], wr.at[part], w_s.at[h], w_r.at[h], groups[1], r)

    def wa_copy(h, n, j):
        part = (pl.ds(h, n), g)
        return remote(wa.at[part], wa.at[part], wa_s.at[h], wa_r.at[h], groups[j], r)

    def wa_all(h, n):
        part = (pl.ds(h, n), pl.ds(0, GRPS - 1))
        return remote(wa.at[part], wa.at[part], wa_s.at[h], wa_r.at[h], groups[1], r)

    def kv_send(h, n):
        each(PEERS, lambda j: kv_copy(h, n, j).start())

    def kv_relay(h, n):
        kv_all(h, n).wait_recv()
        kv_mate(h, n, core).start()

    def project(h):
        for c in w_loads(h):
            c.wait()
        kv[h, mine] = dot(x[...], w[h], NN).astype(BF)

    loads[0].wait()
    project(0)
    pl.semaphore_wait(barrier, 15 + GRPS - 1)
    kv_send(0, 1)
    project(1)

    for c in loads[1:]:
        c.wait()
    row = lax.broadcasted_iota(jnp.int32, (SEQ, D), 0)
    for n in range(2):
        live = jnp.broadcast_to(mask_ref[n:n + 1, :].astype(F32), (SEQ, SEQ)).T
        live = (live == 1.0) & (row < len_ref[n])
        rows = slice(n * SEQ, (n + 1) * SEQ)

        def clear(c, _, rows=rows, live=live):
            cols = lanes(c * D)
            d[rows, cols] = jnp.where(live, d[rows, cols].astype(F32), 0.0).astype(BF)
            return _

        lax.fori_loop(0, HEADS * PER, clear, 0)
    xr[at] = x[:, x_cols(at)]
    xacc[...] = jnp.zeros_like(xacc)

    project(2)
    kv_relay(0, 1)
    kv_send(1, 1)
    project(3)

    causal = (lax.broadcasted_iota(jnp.int32, (ROWS, SEQ), 1)
              <= lax.broadcasted_iota(jnp.int32, (ROWS, SEQ), 0) % SEQ)

    def own_kv(h, n):
        rows = slice(n * SEQ, (n + 1) * SEQ)
        return own[rows, lanes(h * D)], own[rows, lanes(512 + h * D)]

    def kept(h, n):
        return (h % KEPT) * 2 + n

    def softmax_part(h, n):
        rows = slice(n * SEQ, (n + 1) * SEQ)
        qn = jnp.concatenate([q[rows, lanes((h * PER + t) * D)] for t in range(PER)], 0)
        dn = jnp.concatenate([d[rows, lanes((h * PER + t) * D)] for t in range(PER)], 0)
        keys = kv[h, :, :, 0:D].reshape(PROMPT, D)
        values = kv[h, :, :, D:].reshape(PROMPT, D)
        ko, vo = own_kv(h, n)
        none = jnp.zeros_like(ko)
        both = jnp.concatenate(
            [jnp.concatenate([ko, none], 1), jnp.concatenate([none, vo], 1)], 0)
        last = dot(jnp.concatenate([qn, dn], 1), both, NT)
        scores = jnp.concatenate(
            [dot(qn, keys, NT), jnp.where(causal, last[:, :SEQ], -1e30)], 1)
        pgrad = jnp.concatenate([dot(dn, values, NT), last[:, SEQ:]], 1)
        top = jnp.max(scores, axis=1, keepdims=True)
        e = jnp.exp2((scores - top) * (SCALE * LOG2E))
        inv = 1.0 / jnp.sum(e, axis=1, keepdims=True)
        center = jnp.sum(e * pgrad, axis=1, keepdims=True) * inv
        es[n] = e.astype(BF)
        ss[kept(h, n)] = (e * ((pgrad - center) * inv)).astype(BF)
        dd[n] = (dn * inv).astype(BF)

    def key_part(h):
        total = []
        for n in range(2):
            rows = slice(n * SEQ, (n + 1) * SEQ)
            qn = jnp.concatenate([q[rows, lanes((h * PER + t) * D)] for t in range(PER)], 0)
            dk = dot(qn, ss[kept(h, n)], TN) * SCALE
            dv = dot(dd[n], es[n], TN)
            own_g[rows, lanes(h * D)] = dk[:, PROMPT:].astype(BF).T
            own_g[rows, lanes(512 + h * D)] = dv[:, PROMPT:].astype(BF).T
            total.append((dk[:, :PROMPT], dv[:, :PROMPT]))
        dk, dv = total[0][0] + total[1][0], total[0][1] + total[1][1]
        pb[h, :, :, 0:D] = dk.astype(BF).T.reshape(16, TOK, D)
        pb[h, :, :, D:] = dv.astype(BF).T.reshape(16, TOK, D)

    def qg_out(h, n):
        part = (pl.ds(n * SEQ, SEQ), lanes(h * PER * D, PER * D))
        return pltpu.make_async_copy(q.at[part], qg_hbm.at[part], qg_sem.at[h, n])

    def query_part(h, n):
        rows = slice(n * SEQ, (n + 1) * SEQ)
        keys = jnp.concatenate([kv[h, :, :, 0:D].reshape(PROMPT, D), own_kv(h, n)[0]], 0)
        out = (dot(ss[kept(h, n)], keys, NN) * SCALE).astype(BF)
        for t in range(PER):
            q[rows, lanes((h * PER + t) * D)] = out[t * SEQ:(t + 1) * SEQ]
        qg_out(h, n).start()

    def pair_sum(h):
        p_copy(h).wait_recv()
        half = pb[h, pl.ds(core * PEERS, PEERS)].astype(F32) + pr[h].astype(F32)
        pb[h, pl.ds(core * PEERS, PEERS)] = half.astype(BF)
        each(PEERS, lambda j: rs_copy(h, j).start())
        rsr[h, at] = pb[h, mine]

    def group_sum(h):
        rs_all(h).wait_recv()
        total = rsr[h, 0].astype(F32)
        for j in range(1, PEERS):
            total += rsr[h, j].astype(F32)
        ga[h, at] = total.astype(BF)
        each(PEERS, lambda j: ga_copy(h, j).start())

    def x_part(h):
        def tile(c, _):
            rows = pl.ds(c * 1024, 1024)
            xacc[:, lanes(c * 1024, 1024)] += dot(ga[h, at], w[h, rows, :], NT)
            return _

        lax.fori_loop(0, WIDTH // 1024, tile, 0)

    def w_part(h):
        part = dot(xr[...].reshape(PEERS * TOK, 2 * WROWS), ga[h].reshape(PEERS * TOK, 2 * D), TN)
        low, high = part[:WROWS], part[WROWS:]
        wf[h] = jnp.where(core == 0, high, low).astype(BF)
        wo[h % 2] = jnp.where(core == 0, low, high)

    def w_send(h, n):
        for i in range(h, h + n):
            ga_all(i).wait_recv()
            w_part(i)
        wp_copy(h, n).start()

    def w_pair(h, n):
        wp_copy(h, n).wait_recv()
        for k in range(h, h + n):
            part = (wo[k % 2] + wp[k].astype(F32)).astype(BF)
            for i in range(4):
                for t in range(2):
                    ws[k, i * 2 + t] = part[i * WPART:(i + 1) * WPART, t * D:(t + 1) * D]
        each(GRPS, lambda j: w_copy(h, n, j).start())
        for k in range(h, h + n):
            wr[k, g] = ws[k, g]

    def w_sum(h, n):
        w_all(h, n).wait_recv()
        for k in range(h, h + n):
            total = wr[k, 0].astype(F32)
            for j in range(1, GRPS):
                total += wr[k, j].astype(F32)
            wa[k, g] = total.astype(BF)
        each(GRPS, lambda j: wa_copy(h, n, j).start())

    def wa_out(h, n):
        part = pl.ds(h, n)
        return pltpu.make_async_copy(wa.at[part], wa_hbm.at[part], out_sem.at[2 + h])

    def w_out(h, n):
        wa_all(h, n).wait_recv()
        wa_out(h, n).start()

    def when(cond):
        return pl.when(cond) if not isinstance(cond, bool) else (lambda f: f() if cond else None)

    def head(h, c):
        @when(h < 2)
        def _():
            kv_mate(h, 1, 1 - core).wait_recv()

        @when(h == 2)
        def _():
            kv_mate(2, 2, 1 - core).wait_recv()

        softmax_part(h, 0)

        @when(h >= 1)
        def _():
            pair_sum(h - 1)

        @when(h == 0)
        def _():
            kv_send(2, 2)

        softmax_part(h, 1)

        @when(h == 0)
        def _():
            kv_relay(1, 1)

        @when(h == 1)
        def _():
            kv_relay(2, 2)

        @when(h == 2)
        def _():
            group_sum(0)

        key_part(h)
        p_copy(h).start()

        @when(h == 0)
        def _():
            each(PEERS, lambda j: x_copy(j).start())

        return c

    lax.fori_loop(0, HEADS, head, 0)

    own_out = pltpu.make_async_copy(own_g, own_hbm, out_sem.at[0])
    xg_out = pltpu.make_async_copy(x, xg_hbm, out_sem.at[1])
    own_out.start()
    group_sum(1)
    pair_sum(3)
    group_sum(2)
    query_part(0, 0)
    query_part(0, 1)
    x_all().wait_recv()
    x_part(0)
    w_send(0, 2)
    query_part(1, 0)
    w_pair(0, 2)
    group_sum(3)
    query_part(1, 1)
    w_send(2, 1)
    x_part(1)
    w_pair(2, 1)
    query_part(2, 0)
    w_send(3, 1)
    w_sum(0, 2)
    w_pair(3, 1)
    query_part(2, 1)
    x_part(2)
    w_sum(2, 1)
    query_part(3, 0)
    w_sum(3, 1)
    query_part(3, 1)
    x_part(3)
    x_all().wait_send()
    x[...] = xacc[...].astype(BF)
    xg_out.start()
    w_out(0, 2)

    for h in range(HEADS):
        p_copy(h).wait_send()
        rs_all(h).wait_send()
        ga_all(h).wait_send()
        for n in range(2):
            qg_out(h, n).wait()
    for h, n in ((0, 1), (1, 1), (2, 2)):
        kv_all(h, n).wait_send()
        kv_mate(h, n, core).wait_send()
    own_out.wait()
    w_out(2, 1)
    for h, n in ((0, 2), (2, 1), (3, 1)):
        wp_copy(h, n).wait_send()
        w_all(h, n).wait_send()
    xg_out.wait()
    w_out(3, 1)
    for h, n in ((0, 2), (2, 1), (3, 1)):
        wa_all(h, n).wait_send()
        wa_out(h, n).wait()


CHUNKS = 4


def finish(qg_in, own_in, xg_in, wa_in, qg, own_g, xg, wg, qv, ov, xv, wav, wv, in_sem, out_sem):
    size = 2 * SEQ // CHUNKS
    moves = [(wa_in, wav, None)]
    for i in range(CHUNKS):
        part = pl.ds(i * size, size)
        moves.append((qg_in.at[part], qv.at[part], qg.at[part]))
    moves += [(own_in, ov, own_g), (xg_in, xv, xg)]
    ins = [pltpu.make_async_copy(src, mid, in_sem.at[n]) for n, (src, mid, _) in enumerate(moves)]
    outs = [pltpu.make_async_copy(mid, dst, out_sem.at[n])
            for n, (_, mid, dst) in enumerate(moves) if dst is not None]
    w_out = pltpu.make_async_copy(wv, wg, out_sem.at[0])
    for c in ins:
        c.start()
    for c, o in zip(ins[1:], outs):
        c.wait()
        o.start()
    ins[0].wait()
    for h in range(HEADS):
        for i in range(4):
            for t in range(2):
                wv[i * WPART:(i + 1) * WPART, t * 512 + h * D:t * 512 + (h + 1) * D] = (
                    wav[h, i * 2 + t].astype(F32))
    w_out.start()
    w_out.wait()
    for o in outs:
        o.wait()


def local(prompt_x, key_value_weight, queries, resp_kv, out_grad, lengths, token_mask):
    dma = pltpu.SemaphoreType.DMA
    vmem = pl.BlockSpec(memory_space=pltpu.VMEM)
    hbm = pl.BlockSpec(memory_space=pl.ANY)
    pairs = lambda *shape: [dma(shape), dma(shape)]
    qg_shape = jax.ShapeDtypeStruct((2 * SEQ, HEADS * PER * D), BF)
    own_shape = jax.ShapeDtypeStruct((2 * SEQ, 2 * HEADS * D), BF)
    xg_shape = jax.ShapeDtypeStruct((TOK, WIDTH), BF)
    parts = pl.pallas_call(
        kernel,
        out_shape=(
            qg_shape, own_shape, xg_shape,
            jax.ShapeDtypeStruct((HEADS, GRPS, WPART, D), BF),
        ),
        in_specs=[hbm] * 5 + [pl.BlockSpec(memory_space=pltpu.SMEM), vmem],
        out_specs=(hbm,) * 4,
        scratch_shapes=[
            pltpu.VMEM((TOK, WIDTH), BF),
            pltpu.VMEM((HEADS, WIDTH, 2 * D), BF),
            pltpu.VMEM((2 * SEQ, HEADS * PER * D), BF),
            pltpu.VMEM((2 * SEQ, HEADS * PER * D), BF),
            pltpu.VMEM((2 * SEQ, 2 * HEADS * D), BF),
            pltpu.VMEM((2 * SEQ, 2 * HEADS * D), BF),
            pltpu.VMEM((HEADS, 16, TOK, 2 * D), BF),
            pltpu.VMEM((HEADS, 16, TOK, 2 * D), BF),
            pltpu.VMEM((HEADS, PEERS, TOK, 2 * D), BF),
            pltpu.VMEM((HEADS, PEERS, TOK, 2 * D), BF),
            pltpu.VMEM((HEADS, PEERS, TOK, 2 * D), BF),
            pltpu.VMEM((PEERS, TOK, 2 * WROWS), BF),
            pltpu.VMEM((HEADS, WROWS, 2 * D), BF),
            pltpu.VMEM((2, WROWS, 2 * D), F32),
            pltpu.VMEM((HEADS, WROWS, 2 * D), BF),
            pltpu.VMEM((HEADS, GRPS, WPART, D), BF),
            pltpu.VMEM((HEADS, GRPS, WPART, D), BF),
            pltpu.VMEM((HEADS, GRPS, WPART, D), BF),
            pltpu.VMEM((2, ROWS, KEYS), BF),
            pltpu.VMEM((2 * KEPT, ROWS, KEYS), BF),
            pltpu.VMEM((2, ROWS, D), BF),
            pltpu.VMEM((TOK, WIDTH), F32),
            dma((4,)),
            dma((HEADS, 2)),
            dma((HEADS, 2)),
            dma((2 + HEADS,)),
            *pairs(HEADS),
            *pairs(HEADS),
            *pairs(HEADS),
            *pairs(HEADS),
            *pairs(HEADS),
            *pairs(1),
            *pairs(HEADS),
            *pairs(HEADS),
            *pairs(HEADS),
        ],
        compiler_params=pltpu.CompilerParams(
            collective_id=0, has_side_effects=True, vmem_limit_bytes=64 << 20
        ),
    )(prompt_x, key_value_weight, queries, resp_kv, out_grad, lengths, token_mask)
    return pl.pallas_call(
        finish,
        out_shape=(
            qg_shape, own_shape, xg_shape,
            jax.ShapeDtypeStruct((WROWS, 2 * HEADS * D), F32),
        ),
        in_specs=[hbm] * 4,
        out_specs=(hbm,) * 4,
        scratch_shapes=[
            pltpu.VMEM(qg_shape.shape, BF),
            pltpu.VMEM(own_shape.shape, BF),
            pltpu.VMEM(xg_shape.shape, BF),
            pltpu.VMEM((HEADS, GRPS, WPART, D), BF),
            pltpu.VMEM((WROWS, 2 * HEADS * D), F32),
            dma((3 + CHUNKS,)),
            dma((3 + CHUNKS,)),
        ],
        compiler_params=pltpu.CompilerParams(vmem_limit_bytes=60 << 20),
    )(*parts)


def solution(mesh):
    rows = P(("grp", "rsp"), None)
    return jax.shard_map(
        local,
        mesh=mesh,
        in_specs=(rows, P(), rows, rows, rows, P(("grp", "rsp")), rows),
        out_specs=(rows, rows, rows, P("rsp", None)),
        check_vma=False,
    )
```
